512 devices in a mesh: ctx: 64 (over z, y), head: 8 (over x, core).
Axes of the slice: x: 4, y: 8, z: 8, core: 2. Of those that a mesh axis runs over, the one named last changes fastest.
Arguments:
- query_rows: bfloat16 [8192, 4096], P('ctx', 'head'), may hold values from -6 to 6
- key_rows: bfloat16 [8192, 4096], P('ctx', 'head'), may hold values from -6 to 6
- value_rows: bfloat16 [8192, 4096], P('ctx', 'head'), may hold values from -6 to 6
- decay_rates: float32 [8192, 32], P('ctx', 'head'), may hold values from 0 to 0.6, as said below
- beta_rates: float32 [8192, 32], P('ctx', 'head'), may hold values from 0 to 1
- level_weights: float32 [8192, 32, 7], P('ctx', 'head'), may hold values from 0.5 to 8
- out_weight: bfloat16 [4096, 4096], P('head', 'ctx'), may hold values from -0.09375 to 0.09375
Outputs:
- mixed: bfloat16 [8192, 4096], P('ctx', 'head')
The draws below stay inside these ranges and needn't reach their ends.
Inputs may be any that keep to these rules, and one draw needn't show every extreme that they name: `decay_rates`: non-negative decay rate per token and head.
All inputs are finite; a program needn't handle non-finite values.
Results may differ from the reference program's by a relative error of at most 0.017.
Values may be sent and summed in bfloat16 or wider, within the bound.
A program may use at most 64 MiB of HBM per device.

```python
import math
import jax
import jax.numpy as jnp
from jax import lax

D = 4096
H = 32
DK = 128
CH = 64
TOK_DEV = 128
WINDOW_TOKENS = 8192
LEVELS = 7
N_HEAD = 8


def slow_heads(key, share):
    return (jax.random.uniform(key, (H,)) < share).astype(jnp.float32)


def draw_decay_rates(key, part):
    slow_flag = slow_heads(key, 0.5)
    lower_end = 0.5
    upper_end = 1.5
    key = jax.random.fold_in(key, 11)
    key_block, key_token, key_offsets, key_lengths = jax.random.split(key, 4)
    blocks = WINDOW_TOKENS // TOK_DEV
    rate_base = slow_flag * (0.3 / WINDOW_TOKENS) + (1.0 - slow_flag) * (1.0 / 40.0)
    per_block = jnp.exp(jax.random.uniform(key_block, (blocks, 1, H), minval=-0.7, maxval=0.7))
    per_token = jax.random.uniform(key_token, (blocks, TOK_DEV, H), minval=lower_end, maxval=upper_end)
    rate_values = (rate_base * per_block * per_token).reshape(WINDOW_TOKENS, H)
    segment_offsets = jax.random.randint(key_offsets, (3,), 0, WINDOW_TOKENS)
    segment_lengths = jax.random.uniform(key_lengths, (3,), minval=0.22, maxval=0.5)
    segment_matches = (jnp.arange(WINDOW_TOKENS)[:, None] == segment_offsets[None, :]).astype(jnp.float32)
    segment_list = jnp.sum(segment_matches * segment_lengths[None, :], axis=1)
    return (rate_values + segment_list[:, None]).astype(jnp.float32)


def draw_beta_rates(key, part):
    slow_flag = slow_heads(key, 0.5)
    key = jax.random.fold_in(key, 12)
    key_fast, key_slow = jax.random.split(key, 2)
    fast_value = jax.random.uniform(key_fast, (WINDOW_TOKENS, H), minval=0.1, maxval=0.9)
    slow_value = DK / WINDOW_TOKENS * jax.random.uniform(key_slow, (WINDOW_TOKENS, H), minval=0.3, maxval=0.9)
    return (slow_flag * slow_value + (1.0 - slow_flag) * fast_value).astype(jnp.float32)


def level_of(stream_key, dims, cuts, smallest, high):
    def one(dim, shards_of):
        draws = jax.random.uniform(jax.random.fold_in(jax.random.fold_in(stream_key, 6), dim), (shards_of,), jnp.float32, smallest / len(cuts), high / len(cuts))
        return jnp.repeat(jnp.exp(draws), dims[dim] // shards_of).reshape((-1,) + (1,) * (len(dims) - dim - 1))

    loudness = one(*cuts[0])
    for cut in cuts[1:]:
        loudness = loudness * one(*cut)
    return loudness


def centred(own_key, extent, spread, limit, cuts=(), kind=jnp.bfloat16):
    values = jax.random.normal(own_key, extent, jnp.float32) * spread
    if len(cuts) > 0:
        values = level_of(own_key, extent, cuts, -0.22, 0.18) * values
    return jnp.clip(values, min=-limit, max=limit).astype(kind)


def setup_inputs(seed: int = 0) -> dict:
    streams_of = jax.random.split(jax.random.key(seed), 8)
    return {
        "query_rows": centred(streams_of[0], (WINDOW_TOKENS, H * DK), 1.0, 6.0, ((0, 64), (1, 8))),
        "key_rows": centred(streams_of[1], (WINDOW_TOKENS, H * DK), 1.0, 6.0, ((0, 64), (1, 8))),
        "value_rows": centred(streams_of[2], (WINDOW_TOKENS, H * DK), 1.0, 6.0, ((0, 64), (1, 8))),
        "decay_rates": draw_decay_rates(jax.random.fold_in(streams_of[7], 71), 0),
        "beta_rates": draw_beta_rates(jax.random.fold_in(streams_of[7], 71), 0),
        "level_weights": jnp.clip(jnp.exp(math.log(8.0) - 2.7725887 * jax.random.uniform(streams_of[5], (WINDOW_TOKENS, H, LEVELS), jnp.float32) ** level_of(streams_of[5], (WINDOW_TOKENS, H, LEVELS), ((0, 64), (1, 8)), -0.2, 0.2)), 0.5, 8.0),
        "out_weight": centred(streams_of[6], (H * DK, D), (H * DK) ** -0.5, 0.09375, ((0, 8), (1, 64))),
    }


topmost_level = lax.Precision.HIGHEST

def unit_rows(vectors):
    return vectors * lax.rsqrt(lax.optimization_barrier(jnp.sum(vectors * vectors, axis=-1, keepdims=True)) + 1e-06)

def span_terms(queries, key_vecs, value_vecs, decay_vals, beta_vals):
    length = queries.shape[-2]
    key_width = queries.shape[-1]
    lower_ones = jnp.tril(jnp.ones((length, length), jnp.float32))
    inside = lower_ones > 0.5
    strict = jnp.tril(jnp.ones((length, length), jnp.float32), -1) > 0.5
    cumulative = -jnp.einsum('...s,ts->...t', decay_vals, lower_ones, precision=topmost_level)
    growth = jnp.exp(cumulative)
    gap_matrix = cumulative[..., :, None] - cumulative[..., None, :]
    ratios = jnp.where(inside, jnp.exp(jnp.minimum(gap_matrix, 0.0)), 0.0)
    key_key = jnp.einsum('...td,...sd->...ts', key_vecs, key_vecs, precision=topmost_level)
    query_key = jnp.einsum('...td,...sd->...ts', queries, key_vecs, precision=topmost_level)
    coupling = jnp.where(strict, beta_vals[..., :, None] * ratios * key_key, 0.0)
    system = coupling + jnp.eye(length, dtype=jnp.float32)
    right_side = jnp.concatenate([(beta_vals * growth)[..., None] * key_vecs, beta_vals[..., None] * value_vecs], axis=-1)
    solved = jax.scipy.linalg.solve_triangular(system, right_side, lower=True, unit_diagonal=True)
    weight_rows = solved[..., :key_width]
    updates = solved[..., key_width:]
    scores = query_key * ratios
    inner_out = jnp.einsum('...ts,...sv->...tv', scores, updates, precision=topmost_level)
    moved_queries = growth[..., None] * queries - jnp.einsum('...ts,...sk->...tk', scores, weight_rows, precision=topmost_level)
    final_log = cumulative[..., -1:]
    tail_keys = jnp.exp(final_log - cumulative)[..., None] * key_vecs
    transition = jnp.exp(final_log)[..., None] * jnp.eye(key_width, dtype=jnp.float32) - jnp.einsum('...sk,...sj->...kj', tail_keys, weight_rows, precision=topmost_level)
    injection = jnp.einsum('...sk,...sv->...kv', tail_keys, updates, precision=topmost_level)
    return (transition, injection, moved_queries, inner_out)

def block_terms(queries, key_vecs, value_vecs, decay_vals, beta_vals):
    transition, injection, moved_queries, inner_out = span_terms(queries, key_vecs, value_vecs, decay_vals, beta_vals)
    key_width = queries.shape[-1]
    batch_shape = transition.shape[:-3]
    start_map = jnp.broadcast_to(jnp.eye(key_width, dtype=jnp.float32), batch_shape + (key_width, key_width))
    start_add = jnp.zeros(batch_shape + (key_width, value_vecs.shape[-1]), jnp.float32)

    def advance(carried_pair, span_items):
        prefix_map, prefix_add = carried_pair
        span_map, span_add, span_queries, span_inner = span_items
        local_out = span_inner + jnp.einsum('...tk,...kv->...tv', span_queries, prefix_add, precision=topmost_level)
        raised_values = jnp.einsum('...tk,...kj->...tj', span_queries, prefix_map, precision=topmost_level)
        next_map = jnp.einsum('...ij,...jk->...ik', span_map, prefix_map, precision=topmost_level)
        next_add = jnp.einsum('...ij,...jv->...iv', span_map, prefix_add, precision=topmost_level) + span_add
        return ((next_map, next_add), (local_out, raised_values))
    span_items = (jnp.moveaxis(transition, -3, 0), jnp.moveaxis(injection, -3, 0), jnp.moveaxis(moved_queries, -3, 0), jnp.moveaxis(inner_out, -3, 0))
    (block_map, block_add), (local_out, raised_values) = lax.scan(advance, (start_map, start_add), span_items)
    return (block_map, block_add, jnp.moveaxis(local_out, 0, -3), jnp.moveaxis(raised_values, 0, -3))

def head_output(head_items):
    queries, key_vecs, value_vecs, decay_vals, beta_vals, weight_vals = head_items
    blocks = WINDOW_TOKENS // TOK_DEV
    sub_count = TOK_DEV // CH
    level_count = LEVELS - 1
    queries = unit_rows(queries.astype(jnp.float32)).reshape(blocks, sub_count, CH, DK)
    key_vecs = unit_rows(key_vecs.astype(jnp.float32)).reshape(blocks, sub_count, CH, DK)
    value_vecs = value_vecs.astype(jnp.float32).reshape(blocks, sub_count, CH, DK)
    decay_vals = decay_vals.reshape(blocks, sub_count, CH)
    beta_vals = beta_vals.reshape(blocks, sub_count, CH)
    weight_vals = weight_vals.reshape(blocks, sub_count, CH, LEVELS)
    block_map, block_add, local_out, raised_values = block_terms(queries, key_vecs, value_vecs, decay_vals, beta_vals)
    level_ids = jnp.arange(level_count, dtype=jnp.int32)
    powers = 2 ** level_ids

    def advance(states, block_items):
        span_map, span_add, position = block_items
        bit_values = position // powers % 2
        trailing = jnp.sum(jnp.cumprod(bit_values))
        below_mask = (level_ids < trailing).astype(jnp.float32)
        merged = jnp.einsum('kj,jv->kv', span_map, lax.optimization_barrier(jnp.sum(states * below_mask[:, None, None], axis=0)), precision=topmost_level) + span_add
        carried = jnp.einsum('kj,ljv->lkv', span_map, states, precision=topmost_level)
        target = (level_ids == trailing)[:, None, None]
        above_mask = (level_ids > trailing)[:, None, None]
        updated = jnp.where(target, merged[None], jnp.where(above_mask, carried, 0.0))
        return (updated, states)
    start_states = jnp.zeros((level_count, DK, DK), jnp.float32)
    _, level_states = lax.scan(advance, start_states, (block_map, block_add, jnp.arange(blocks, dtype=jnp.int32)))
    far_terms = jnp.einsum('bsck,blkv,bscl->bscv', raised_values, level_states, weight_vals[..., 1:], precision=topmost_level)
    result = weight_vals[..., 0:1] * local_out + far_terms
    return result.reshape(WINDOW_TOKENS, DK)

def reference(query_rows, key_rows, value_rows, decay_rates, beta_rates, level_weights, out_weight):
    heads_q = query_rows.reshape(WINDOW_TOKENS, H, DK).transpose(1, 0, 2)
    heads_k = key_rows.reshape(WINDOW_TOKENS, H, DK).transpose(1, 0, 2)
    heads_v = value_rows.reshape(WINDOW_TOKENS, H, DK).transpose(1, 0, 2)
    mixer_out = lax.map(head_output, (heads_q, heads_k, heads_v, decay_rates.T, beta_rates.T, level_weights.transpose(1, 0, 2)))
    mixer_out = mixer_out.transpose(1, 0, 2).reshape(WINDOW_TOKENS, H * DK).astype(jnp.bfloat16)
    group_rows = H * DK // N_HEAD
    summed = jnp.zeros((WINDOW_TOKENS, D), jnp.float32)
    for group_index in range(N_HEAD):
        lower_row = group_index * group_rows
        partial_value = jnp.dot(mixer_out[:, lower_row:lower_row + group_rows].astype(jnp.float32), out_weight[lower_row:lower_row + group_rows].astype(jnp.float32), preferred_element_type=jnp.float32).astype(jnp.bfloat16)
        partial_value = lax.optimization_barrier(partial_value)
        summed = summed + partial_value.astype(jnp.float32)
    return summed.astype(jnp.bfloat16)
```

```python
import jax
import jax.numpy as jnp
from jax import lax
from jax.sharding import PartitionSpec as P
from jax.experimental import pallas as pl
from jax.experimental.pallas import tpu as pltpu

DK = 128
TB = 128
MESH = pl.DeviceIdType.MESH
F32 = jnp.float32
BF16 = jnp.bfloat16


def split(a):
    hi = a.astype(BF16)
    lo = (a - hi.astype(F32)).astype(BF16)
    return hi, lo


def dot3(a, b):
    ah, al = split(a)
    bh, bl = split(b)
    return jnp.dot(
        jnp.concatenate([ah, ah, al], axis=1),
        jnp.concatenate([bh, bl, bh], axis=0),
        preferred_element_type=F32,
    )


def dot3_nt(a, b):
    ah, al = split(a)
    bh, bl = split(b)
    return lax.dot_general(
        jnp.concatenate([ah, ah, al], axis=1),
        jnp.concatenate([bh, bl, bh], axis=1),
        (((1,), (1,)), ((), ())),
        preferred_element_type=F32,
    )


def unit_rows(x):
    return x * lax.rsqrt(jnp.sum(x * x, axis=-1, keepdims=True) + 1e-06)


def kernel(
    q_ref, k_ref, v_ref, dec_ref, beta_ref, lw_ref, w_ref, out_ref,
    small, rq, rk, rv, rs, kn, gm, wu, ab, cols, lrt, ot, tot, relay,
    st_send, st_recv, osend, mt, wg, acc, sib_send, sib_recv, x_send, x_recv,
    kv_ss, kv_rs, q_ss, q_rs, st_ss, st_rs, o_ss, o_rs, w1_ss, w1_rs, w2_ss, w2_rs,
    sb_ss, sb_rs, x_ss, x_rs,
):
    ctx = lax.axis_index("ctx")
    head = lax.axis_index("head")
    zi = ctx // 8
    yi = ctx % 8
    yl = ctx % 4
    base = ctx - yl
    core = head % 2
    xi = head // 2

    def at_zy(z, y):
        return {"ctx": z * 8 + y}

    barrier = pltpu.get_barrier_semaphore()
    for d in range(1, 8):
        pl.semaphore_signal(barrier, inc=1, device_id=at_zy(zi, (yi + d) % 8), device_id_type=MESH)
        pl.semaphore_signal(barrier, inc=1, device_id=at_zy((zi + d) % 8, yi), device_id_type=MESH)
    for d in range(1, 4):
        pl.semaphore_signal(
            barrier, inc=1, device_id={"head": ((xi + d) % 4) * 2 + core}, device_id_type=MESH
        )
    pl.semaphore_signal(barrier, inc=1, device_id={"head": head ^ 1}, device_id_type=MESH)

    pack = jnp.concatenate(
        [dec_ref[...], beta_ref[...], lw_ref[...], jnp.zeros((TB, 92), F32)], axis=1
    ).T
    for j in range(4):
        small[j, 0:1, :] = pack[j : j + 1]
        small[j, 1:2, :] = pack[4 + j : 5 + j]
        small[j, 2:9, :] = pack[8 + 7 * j : 15 + 7 * j]
        small[j, 9:16, :] = jnp.zeros((7, TB), F32)
    wg[zi, yi] = w_ref[...].astype(F32).T.astype(BF16)

    pl.semaphore_wait(barrier, 18)

    def lane(j):
        return pl.ds(pl.multiple_of(j * DK, DK), DK)

    kv_copies = []
    for d in (3, 2, 1):
        to = (yl + d) % 4
        for a, (src, dst) in enumerate(
            ((k_ref.at[:, lane(to)], rk), (v_ref.at[:, lane(to)], rv), (small.at[to], rs))
        ):
            cp = pltpu.make_async_remote_copy(
                src_ref=src, dst_ref=dst.at[yl], send_sem=kv_ss.at[a, d], recv_sem=kv_rs.at[a, d],
                device_id={"ctx": base + to}, device_id_type=MESH,
            )
            cp.start()
            kv_copies.append(cp)

    def w1_copy(half, d):
        to = at_zy((zi + d) % 8, yi) if half == 0 else at_zy(zi, (yi + d) % 8)
        part = wg.at[zi, yi, pl.ds(32 * half, 32)]
        return pltpu.make_async_remote_copy(
            src_ref=part, dst_ref=part, send_sem=w1_ss.at[half, d], recv_sem=w1_rs.at[half, d],
            device_id=to, device_id_type=MESH,
        )

    w1 = [[w1_copy(half, d) for d in range(1, 8)] for half in range(2)]
    for cp in w1[0]:
        cp.start()

    def w2_copy(half, way, step):
        mine = yi if half == 0 else zi
        slot = (mine + (-(step - 1) if way == 0 else step - 1) + 8) % 8
        nxt = (mine + (1 if way == 0 else 7)) % 8
        to = at_zy(zi, nxt) if half == 0 else at_zy(nxt, yi)
        low = 32 * half
        size = 32
        if step == 4:
            low = low + 16 * way
            size = 16
        part = wg.at[:, slot, pl.ds(low, size)] if half == 0 else wg.at[slot, :, pl.ds(low, size)]
        return pltpu.make_async_remote_copy(
            src_ref=part, dst_ref=part,
            send_sem=w2_ss.at[half, way, step], recv_sem=w2_rs.at[half, way, step],
            device_id=to, device_id_type=MESH,
        )

    w2 = [[[w2_copy(h, w, s) for s in range(1, 5)] for w in range(2)] for h in range(2)]

    def w2_start(half, step):
        for way in range(2):
            w2[half][way][step - 1].start()

    def w2_wait(half, step):
        for way in range(2):
            w2[half][way][step - 1].wait_recv()

    rq[yl] = q_ref[:, lane(yl)]
    rk[yl] = k_ref[:, lane(yl)]
    rv[yl] = v_ref[:, lane(yl)]
    rs[yl] = small[yl]

    ri = lax.broadcasted_iota(jnp.int32, (TB, TB), 0)
    ci = lax.broadcasted_iota(jnp.int32, (TB, TB), 1)
    eye = (ri == ci).astype(F32)
    upto = (ri <= ci).astype(F32)

    def pairs(slots):
        n = len(slots)
        ls, rhs, keys, tails, lasts = [], [], [], [], []
        for s in slots:
            sm = rs[s]
            g_rows = -jnp.dot(
                sm, upto, preferred_element_type=F32, precision=lax.Precision.HIGHEST
            )
            g_row = g_rows[0:1]
            col = jnp.concatenate([g_row, sm[1:8]], axis=0)
            col = jnp.concatenate([col, jnp.zeros((TB - 8, TB), F32)], axis=0).T
            g_col = col[:, 0:1]
            b_col = col[:, 1:2]
            growth = jnp.exp(g_col)
            g_last = g_row[:, TB - 1 : TB]
            ratio = jnp.where(ci <= ri, jnp.exp(jnp.minimum(g_col - g_row, 0.0)), 0.0)
            kk = unit_rows(rk[s].astype(F32))
            kn[s] = kk
            gm[s] = ratio
            cols[s] = jnp.broadcast_to(growth, (TB, DK))
            ls.append(jnp.where(ci < ri, b_col * ratio * dot3_nt(kk, kk), 0.0))
            rhs.append(
                jnp.concatenate([(b_col * growth) * kk, b_col * rv[s].astype(F32)], axis=1)
            )
            tails.append(jnp.exp(g_last - g_col) * kk)
            lasts.append(jnp.exp(g_last))
        inv = [eye - jnp.where((ri % 2 == 1) & (ci == ri - 1), l, 0.0) for l in ls]
        b = 2
        while b < TB:
            mask = ((ri // b) % 2 == 1) & (ci // b == ri // b - 1)
            mid = [dot3(inv[i], jnp.where(mask, ls[i], 0.0)) for i in range(n)]
            inv = [inv[i] - dot3(mid[i], inv[i]) for i in range(n)]
            b *= 2
        sol = [dot3(inv[i], rhs[i]) for i in range(n)]
        for i, s in enumerate(slots):
            wu[s] = sol[i]
            m = dot3(tails[i].T, sol[i])
            ab[s, :, 0:DK] = lasts[i] * eye - m[:, 0:DK]
            ab[s, :, DK:] = m[:, DK:]

    pairs([yl])

    for cp in kv_copies:
        cp.wait_recv()
    q_copies = []
    for d in (3, 2, 1):
        to = (yl + d) % 4
        cp = pltpu.make_async_remote_copy(
            src_ref=q_ref.at[:, lane(to)], dst_ref=rq.at[yl], send_sem=q_ss.at[d], recv_sem=q_rs.at[d],
            device_id={"ctx": base + to}, device_id_type=MESH,
        )
        cp.start()
        q_copies.append(cp)
    for cp in w1[1]:
        cp.start()

    pairs([(yl + d) % 4 for d in range(1, 4)])

    def apply(second, first):
        r = dot3(second[:, 0:DK], first)
        return jnp.concatenate([r[:, 0:DK], r[:, DK:] + second[:, DK:]], axis=1)

    ab01 = apply(ab[1], ab[0])
    ab23 = apply(ab[3], ab[2])
    group = apply(ab23, ab01)

    def level_copy(i):
        if i < 3:
            src, dst = st_send.at[i], st_recv.at[i]
        else:
            src, dst = st_send.at[i, :, pl.ds(DK, DK)], st_recv.at[i, :, pl.ds(DK, DK)]
        return pltpu.make_async_remote_copy(
            src_ref=src, dst_ref=dst, send_sem=st_ss.at[i], recv_sem=st_rs.at[i],
            device_id={"ctx": ctx ^ (4 << i)}, device_id_type=MESH,
        )

    levels = [level_copy(i) for i in range(4)]
    tot[...] = group
    st_send[0] = group.astype(BF16)
    levels[0].start()
    relay[...] = eye

    for cp in w1[0]:
        cp.wait_recv()
    w2_start(0, 1)

    for cp in q_copies:
        cp.wait_recv()
    b01 = ab01[:, DK:]
    a2 = ab[2, :, 0:DK]
    r3 = dot3(a2, ab01)
    starts = [None, ab[0, :, 0:DK], ab01[:, 0:DK], r3[:, 0:DK]]
    for s in range(4):
        kk = kn[s]
        qq = unit_rows(rq[s].astype(F32))
        p = dot3_nt(qq, kk) * gm[s]
        pwu = dot3(p, wu[s])
        moved = cols[s] * qq - pwu[:, 0:DK]
        inner = pwu[:, DK:]
        wt = rs[s]
        o = wt[2:3] * inner.T
        if s == 0:
            lifted = moved
        elif s == 1:
            r = dot3(moved, ab[0])
            lifted = r[:, 0:DK]
            o = o + wt[3:4] * r[:, DK:].T
        elif s == 2:
            r = dot3(moved, ab01)
            lifted = r[:, 0:DK]
            o = o + wt[4:5] * r[:, DK:].T
        else:
            r = dot3(moved, jnp.concatenate([r3, ab[2, :, DK:]], axis=1))
            lifted = r[:, 0:DK]
            o = o + wt[4:5] * r[:, DK : 2 * DK].T + wt[3:4] * r[:, 2 * DK :].T
        lrt[:, s * TB : (s + 1) * TB] = lifted.T
        ot[:, s * TB : (s + 1) * TB] = o

    def add_level(i, state):
        t = dot3(state.T, lrt[...])
        for s in range(4):
            sl = slice(s * TB, (s + 1) * TB)
            ot[:, sl] = ot[:, sl] + rs[s, 4 + i + 1 : 4 + i + 2, :] * t[:, sl]

    for cp in w1[1]:
        cp.wait_recv()
    w2_start(1, 1)

    for i in range(4):
        upper = (ctx // (4 << i)) % 2 == 1
        if i < 3:
            levels[i].wait_recv()
            other = st_recv[i].astype(F32)
            own = tot[...]
            first = jnp.where(upper, other, own)
            second = jnp.where(upper, own, other)
            old = relay[...]
            r = dot3(jnp.concatenate([second[:, 0:DK], old], axis=0), first)
            new_b = r[0:DK, DK:] + second[:, DK:]
            tot[:, 0:DK] = r[0:DK, 0:DK]
            tot[:, DK:] = new_b
            st_send[i + 1, :, 0:DK] = r[0:DK, 0:DK].astype(BF16)
            st_send[i + 1, :, DK:] = new_b.astype(BF16)
            if i < 2:
                levels[i + 1].start()
            else:
                @pl.when((ctx // 32) % 2 == 0)
                def _():
                    levels[3].start()
            relay[...] = jnp.where(upper, r[DK:, 0:DK], old)

            @pl.when(upper)
            def _():
                add_level(i, r[DK:, DK:])

            w2_wait(0, i + 1)
            w2_start(0, i + 2)
            w2_wait(1, i + 1)
            w2_start(1, i + 2)
        else:
            @pl.when(upper)
            def _():
                levels[3].wait_recv()
                add_level(3, dot3(relay[...], st_recv[3, :, DK:].astype(F32)))

            @pl.when(jnp.logical_not(upper))
            def _():
                levels[3].wait_send()

    osend[...] = ot[...].astype(BF16)
    o_copies = []
    for d in (3, 2, 1):
        to = (yl + d) % 4
        cp = pltpu.make_async_remote_copy(
            src_ref=osend.at[:, lane(to)], dst_ref=mt.at[pl.ds(pl.multiple_of(yl * DK, DK), DK)],
            send_sem=o_ss.at[d], recv_sem=o_rs.at[d],
            device_id={"ctx": base + to}, device_id_type=MESH,
        )
        cp.start()
        o_copies.append(cp)
    mt[pl.ds(pl.multiple_of(yl * DK, DK), DK)] = osend[:, lane(yl)]
    w2_wait(0, 4)
    w2_wait(1, 4)
    for cp in o_copies:
        cp.wait_recv()

    def share(block):
        w = wg[block].reshape(512, 512)
        return jnp.dot(w, mt[...], preferred_element_type=F32)

    order = (2, 1, 3, 0)
    sib = []
    for j, d in enumerate(order):
        sib_send[j] = share(((xi + d) % 4) * 2 + 1 - core).astype(BF16)
        cp = pltpu.make_async_remote_copy(
            src_ref=sib_send.at[j], dst_ref=sib_recv.at[j], send_sem=sb_ss.at[j], recv_sem=sb_rs.at[j],
            device_id={"head": head ^ 1}, device_id_type=MESH,
        )
        cp.start()
        sib.append(cp)
    xs = []
    for j, d in enumerate(order):
        acc[...] = share(((xi + d) % 4) * 2 + core)
        sib[j].wait_recv()
        total = acc[...] + sib_recv[j].astype(F32)
        if d != 0:
            x_send[d] = total.astype(BF16)
            cp = pltpu.make_async_remote_copy(
                src_ref=x_send.at[d], dst_ref=x_recv.at[d], send_sem=x_ss.at[d], recv_sem=x_rs.at[d],
                device_id={"head": ((xi + d) % 4) * 2 + core}, device_id_type=MESH,
            )
            cp.start()
            xs.append((d, cp))
    for d, cp in xs:
        cp.wait_recv()
        total = total + x_recv[d].astype(F32)
    out_ref[...] = total.T.astype(BF16)

    for cp in kv_copies + q_copies + levels[:3] + o_copies + sib + [c for _, c in xs]:
        cp.wait_send()
    for half in range(2):
        for cp in w1[half]:
            cp.wait_send()
        for way in range(2):
            for cp in w2[half][way]:
                cp.wait_send()


def per_device(q, k, v, dec, beta, lw, w):
    vmem = pl.BlockSpec(memory_space=pltpu.VMEM)
    dma = pltpu.SemaphoreType.DMA
    return pl.pallas_call(
        kernel,
        out_shape=jax.ShapeDtypeStruct((TB, 512), BF16),
        in_specs=[vmem] * 7,
        out_specs=vmem,
        scratch_shapes=[
            pltpu.VMEM((4, 16, TB), F32),
            pltpu.VMEM((4, TB, DK), BF16),
            pltpu.VMEM((4, TB, DK), BF16),
            pltpu.VMEM((4, TB, DK), BF16),
            pltpu.VMEM((4, 16, TB), F32),
            pltpu.VMEM((4, TB, DK), F32),
            pltpu.VMEM((4, TB, TB), F32),
            pltpu.VMEM((4, TB, 2 * DK), F32),
            pltpu.VMEM((4, DK, 2 * DK), F32),
            pltpu.VMEM((4, TB, DK), F32),
            pltpu.VMEM((DK, 4 * TB), F32),
            pltpu.VMEM((DK, 4 * TB), F32),
            pltpu.VMEM((DK, 2 * DK), F32),
            pltpu.VMEM((DK, DK), F32),
            pltpu.VMEM((4, DK, 2 * DK), BF16),
            pltpu.VMEM((4, DK, 2 * DK), BF16),
            pltpu.VMEM((DK, 4 * TB), BF16),
            pltpu.VMEM((4 * DK, TB), BF16),
            pltpu.VMEM((8, 8, 64, 512), BF16),
            pltpu.VMEM((512, TB), F32),
            pltpu.VMEM((4, 512, TB), BF16),
            pltpu.VMEM((4, 512, TB), BF16),
            pltpu.VMEM((4, 512, TB), BF16),
            pltpu.VMEM((4, 512, TB), BF16),
            dma((3, 4)), dma((3, 4)), dma((4,)), dma((4,)), dma((4,)), dma((4,)),
            dma((4,)), dma((4,)), dma((2, 8)), dma((2, 8)), dma((2, 2, 5)), dma((2, 2, 5)),
            dma((4,)), dma((4,)), dma((4,)), dma((4,)),
        ],
        compiler_params=pltpu.CompilerParams(
            collective_id=0, has_side_effects=True, vmem_limit_bytes=40 * 2**20
        ),
        name="mixer",
    )(q, k, v, dec, beta, lw.reshape(TB, 28), w)


def solution(mesh):
    spec = P("ctx", "head")
    return jax.shard_map(
        per_device,
        mesh=mesh,
        in_specs=(spec,) * 5 + (P("ctx", "head", None), P("head", "ctx")),
        out_specs=spec,
        check_vma=False,
    )
```

```python
import jax
import jax.numpy as jnp
from jax import lax
from jax.sharding import PartitionSpec as P
from jax.experimental import pallas as pl
from jax.experimental.pallas import tpu as pltpu

DK = 128
TB = 128
MESH = pl.DeviceIdType.MESH
F32 = jnp.float32
BF16 = jnp.bfloat16


def split(a):
    hi = a.astype(BF16)
    lo = (a - hi.astype(F32)).astype(BF16)
    return hi, lo


def dot3(a, b):
    ah, al = split(a)
    bh, bl = split(b)
    return jnp.dot(
        jnp.concatenate([ah, ah, al], axis=1),
        jnp.concatenate([bh, bl, bh], axis=0),
        preferred_element_type=F32,
    )


def dot3_nt(a, b):
    ah, al = split(a)
    bh, bl = split(b)
    return lax.dot_general(
        jnp.concatenate([ah, ah, al], axis=1),
        jnp.concatenate([bh, bl, bh], axis=1),
        (((1,), (1,)), ((), ())),
        preferred_element_type=F32,
    )


def unit_rows(x):
    return x * lax.rsqrt(jnp.sum(x * x, axis=-1, keepdims=True) + 1e-06)


class Copies:
    def __init__(self):
        self.sends = []
        self.arrivals = []

    def start(self, *copies):
        for cp in copies:
            cp.start()
            self.sends.append(cp)
            self.arrivals.append(cp)

    def arrive(self, *copies):
        for cp in copies:
            cp.wait_recv()
            self.arrivals = [c for c in self.arrivals if c is not cp]

    def finish(self):
        for cp in self.arrivals:
            cp.wait_recv()
        for cp in self.sends:
            cp.wait_send()


def kernel(
    q_ref, k_ref, v_ref, dec_hbm, beta_hbm, lw_hbm, w_ref, out_ref,
    dec_ref, beta_ref, lw_ref, small, rq, rk, rv, rs, kn, gm, wu, ab, cols, lrt, ot, tot, relay,
    st_send, st_recv, mt, wg, sib_send, sib_recv, x_send, x_recv, fsend, fin,
    kv_ss, kv_rs, q_ss, q_rs, st_ss, st_rs, o_ss, o_rs, w1_ss, w1_rs, w2_ss, w2_rs,
    sb_ss, sb_rs, x_ss, x_rs, f_ss, f_rs, in_s,
):
    net = Copies()
    ctx = lax.axis_index("ctx")
    head = lax.axis_index("head")
    zi = ctx // 8
    yi = ctx % 8
    yl = ctx % 4
    yh = yi // 4
    base = ctx - yl
    core = head % 2
    xi = head // 2

    def at_zy(z, y):
        return {"ctx": z * 8 + y}

    def lane(j):
        return pl.ds(pl.multiple_of(j * DK, DK), DK)

    loads = [
        pltpu.make_async_copy(src, dst, in_s.at[i])
        for i, (src, dst) in enumerate(
            (
                (dec_hbm, dec_ref), (beta_hbm, beta_ref), (lw_hbm, lw_ref),
                (w_ref, wg.at[zi, yh]), (k_ref.at[:, lane(yl)], rk.at[yl]),
                (v_ref.at[:, lane(yl)], rv.at[yl]), (q_ref.at[:, lane(yl)], rq.at[yl]),
            )
        )
    ]
    for cp in loads:
        cp.start()

    barrier = pltpu.get_barrier_semaphore()
    for d in range(1, 8):
        pl.semaphore_signal(barrier, inc=1, device_id=at_zy((zi + d) % 8, yi), device_id_type=MESH)
    pl.semaphore_signal(barrier, inc=1, device_id={"ctx": ctx ^ 4}, device_id_type=MESH)
    for d in range(1, 4):
        pl.semaphore_signal(
            barrier, inc=1, device_id={"ctx": base + (yl + d) % 4}, device_id_type=MESH
        )
    for d in range(1, 4):
        pl.semaphore_signal(
            barrier, inc=1, device_id={"head": ((xi + d) % 4) * 2 + core}, device_id_type=MESH
        )
    pl.semaphore_signal(barrier, inc=1, device_id={"head": head ^ 1}, device_id_type=MESH)

    for cp in loads[:3]:
        cp.wait()
    for j in range(4):
        small[j, 0:1, :] = dec_ref[j : j + 1]
        small[j, 1:2, :] = beta_ref[j : j + 1]
        for l in range(7):
            small[j, 2 + l : 3 + l, :] = lw_ref[l, j : j + 1]
        small[j, 9:16, :] = jnp.zeros((7, TB), F32)

    pl.semaphore_wait(barrier, 15)

    kv_copies = []
    for d in (3, 2, 1):
        to = (yl + d) % 4
        for a, (src, dst) in enumerate(
            ((k_ref.at[:, lane(to)], rk), (v_ref.at[:, lane(to)], rv), (small.at[to], rs))
        ):
            cp = pltpu.make_async_remote_copy(
                src_ref=src, dst_ref=dst.at[yl], send_sem=kv_ss.at[a, d], recv_sem=kv_rs.at[a, d],
                device_id={"ctx": base + to}, device_id_type=MESH,
            )
            net.start(cp)
            kv_copies.append(cp)

    loads[3].wait()
    w_pair = pltpu.make_async_remote_copy(
        src_ref=wg.at[zi, yh], dst_ref=wg.at[zi, yh], send_sem=w1_ss, recv_sem=w1_rs,
        device_id={"ctx": ctx ^ 4}, device_id_type=MESH,
    )
    net.start(w_pair)

    def w_copy(way, step):
        slot = (zi + (step - 1) * (2 * way - 1) + 8) % 8
        part = wg.at[slot] if step < 4 else wg.at[slot, way]
        return pltpu.make_async_remote_copy(
            src_ref=part, dst_ref=part, send_sem=w2_ss.at[way, step], recv_sem=w2_rs.at[way, step],
            device_id=at_zy((zi + 1 + 6 * way) % 8, yi), device_id_type=MESH,
        )

    w_ring = [[w_copy(way, step) for way in range(2)] for step in range(1, 5)]

    def w_pass_on(step):
        net.arrive(*w_ring[step - 1])
        net.start(*w_ring[step])

    rs[yl] = small[yl]
    for cp in loads[4:]:
        cp.wait()

    ri = lax.broadcasted_iota(jnp.int32, (TB, TB), 0)
    ci = lax.broadcasted_iota(jnp.int32, (TB, TB), 1)
    eye = (ri == ci).astype(F32)
    upto = (ri <= ci).astype(F32)

    def pairs(slots):
        n = len(slots)
        ls, rhs, keys, tails, lasts = [], [], [], [], []
        for s in slots:
            sm = rs[s]
            g_rows = -jnp.dot(
                sm, upto, preferred_element_type=F32, precision=lax.Precision.HIGHEST
            )
            g_row = g_rows[0:1]
            col = jnp.concatenate([g_row, sm[1:8]], axis=0)
            col = jnp.concatenate([col, jnp.zeros((TB - 8, TB), F32)], axis=0).T
            g_col = col[:, 0:1]
            b_col = col[:, 1:2]
            growth = jnp.exp(g_col)
            g_last = g_row[:, TB - 1 : TB]
            ratio = jnp.where(ci <= ri, jnp.exp(jnp.minimum(g_col - g_row, 0.0)), 0.0)
            kk = unit_rows(rk[s].astype(F32))
            kn[s] = kk
            gm[s] = ratio
            cols[s] = jnp.broadcast_to(growth, (TB, DK))
            ls.append(jnp.where(ci < ri, b_col * ratio * dot3_nt(kk, kk), 0.0))
            rhs.append(
                jnp.concatenate([(b_col * growth) * kk, b_col * rv[s].astype(F32)], axis=1)
            )
            tails.append(jnp.exp(g_last - g_col) * kk)
            lasts.append(jnp.exp(g_last))
        inv = [eye - jnp.where((ri % 2 == 1) & (ci == ri - 1), l, 0.0) for l in ls]
        b = 2
        while b < TB:
            mask = ((ri // b) % 2 == 1) & (ci // b == ri // b - 1)
            mid = [dot3(inv[i], jnp.where(mask, ls[i], 0.0)) for i in range(n)]
            inv = [inv[i] - dot3(mid[i], inv[i]) for i in range(n)]
            b *= 2
        sol = [dot3(inv[i], rhs[i]) for i in range(n)]
        for i, s in enumerate(slots):
            wu[s] = sol[i]
            m = dot3(tails[i].T, sol[i])
            ab[s, :, 0:DK] = lasts[i] * eye - m[:, 0:DK]
            ab[s, :, DK:] = m[:, DK:]

    pairs([yl])
    net.arrive(w_pair)
    net.start(*w_ring[0])

    net.arrive(*kv_copies)
    q_copies = []
    for d in (3, 2, 1):
        to = (yl + d) % 4
        cp = pltpu.make_async_remote_copy(
            src_ref=q_ref.at[:, lane(to)], dst_ref=rq.at[yl], send_sem=q_ss.at[d], recv_sem=q_rs.at[d],
            device_id={"ctx": base + to}, device_id_type=MESH,
        )
        net.start(cp)
        q_copies.append(cp)
    w_pass_on(1)

    pairs([(yl + d) % 4 for d in range(1, 4)])

    def apply(second, first):
        r = dot3(second[:, 0:DK], first)
        return jnp.concatenate([r[:, 0:DK], r[:, DK:] + second[:, DK:]], axis=1)

    ab01 = apply(ab[1], ab[0])
    ab23 = apply(ab[3], ab[2])
    group = apply(ab23, ab01)

    def level_copy(i):
        if i < 3:
            src, dst = st_send.at[i], st_recv.at[i]
        else:
            src, dst = st_send.at[i, :, pl.ds(DK, DK)], st_recv.at[i, :, pl.ds(DK, DK)]
        return pltpu.make_async_remote_copy(
            src_ref=src, dst_ref=dst, send_sem=st_ss.at[i], recv_sem=st_rs.at[i],
            device_id={"ctx": ctx ^ (4 << i)}, device_id_type=MESH,
        )

    levels = [level_copy(i) for i in range(4)]
    tot[...] = group
    st_send[0] = group.astype(BF16)
    net.start(levels[0])
    relay[...] = eye

    net.arrive(*q_copies)
    b01 = ab01[:, DK:]
    a2 = ab[2, :, 0:DK]
    r3 = dot3(a2, ab01)
    starts = [None, ab[0, :, 0:DK], ab01[:, 0:DK], r3[:, 0:DK]]
    for s in range(4):
        kk = kn[s]
        qq = unit_rows(rq[s].astype(F32))
        p = dot3_nt(qq, kk) * gm[s]
        pwu = dot3(p, wu[s])
        moved = cols[s] * qq - pwu[:, 0:DK]
        inner = pwu[:, DK:]
        wt = rs[s]
        o = wt[2:3] * inner.T
        if s == 0:
            lifted = moved
        elif s == 1:
            r = dot3(moved, ab[0])
            lifted = r[:, 0:DK]
            o = o + wt[3:4] * r[:, DK:].T
        elif s == 2:
            r = dot3(moved, ab01)
            lifted = r[:, 0:DK]
            o = o + wt[4:5] * r[:, DK:].T
        else:
            r = dot3(moved, jnp.concatenate([r3, ab[2, :, DK:]], axis=1))
            lifted = r[:, 0:DK]
            o = o + wt[4:5] * r[:, DK : 2 * DK].T + wt[3:4] * r[:, 2 * DK :].T
        lrt[:, s * TB : (s + 1) * TB] = lifted.T
        ot[:, s * TB : (s + 1) * TB] = o

    def add_level(i, state):
        t = dot3(state.T, lrt[...])
        for s in range(4):
            sl = slice(s * TB, (s + 1) * TB)
            ot[:, sl] = ot[:, sl] + rs[s, 4 + i + 1 : 4 + i + 2, :] * t[:, sl]

    w_pass_on(2)

    for i in range(4):
        upper = (ctx // (4 << i)) % 2 == 1
        if i < 3:
            net.arrive(levels[i])
            other = st_recv[i].astype(F32)
            own = tot[...]
            first = jnp.where(upper, other, own)
            second = jnp.where(upper, own, other)
            old = relay[...]
            r = dot3(jnp.concatenate([second[:, 0:DK], old], axis=0), first)
            new_b = r[0:DK, DK:] + second[:, DK:]
            tot[:, 0:DK] = r[0:DK, 0:DK]
            tot[:, DK:] = new_b
            st_send[i + 1, :, 0:DK] = r[0:DK, 0:DK].astype(BF16)
            st_send[i + 1, :, DK:] = new_b.astype(BF16)
            if i < 2:
                net.start(levels[i + 1])
            else:
                @pl.when((ctx // 32) % 2 == 0)
                def _():
                    levels[3].start()
            relay[...] = jnp.where(upper, r[DK:, 0:DK], old)

            @pl.when(upper)
            def _():
                add_level(i, r[DK:, DK:])

            if i == 0:
                w_pass_on(3)
        else:
            @pl.when(upper)
            def _():
                levels[3].wait_recv()
                add_level(3, dot3(relay[...], st_recv[3, :, DK:].astype(F32)))

            @pl.when(jnp.logical_not(upper))
            def _():
                levels[3].wait_send()

    mine = mt.at[pl.ds(pl.multiple_of(yl * DK, DK), DK)]
    mine[...] = ot[...].astype(BF16)
    o_copies = []
    for d in (3, 2, 1):
        cp = pltpu.make_async_remote_copy(
            src_ref=mine, dst_ref=mine, send_sem=o_ss.at[d], recv_sem=o_rs.at[d],
            device_id={"ctx": base + (yl + d) % 4}, device_id_type=MESH,
        )
        net.start(cp)
        o_copies.append(cp)
    net.arrive(*w_ring[3])
    net.arrive(*o_copies)

    def share(block):
        w = wg[block].reshape(128, 512)
        return jnp.dot(w, mt[...], preferred_element_type=F32)

    sib, xs = {}, []

    def to_sibling(d):
        sib_send[d] = share(((xi + d) % 4) * 2 + 1 - core).astype(BF16)
        sib[d] = pltpu.make_async_remote_copy(
            src_ref=sib_send.at[d], dst_ref=sib_recv.at[d], send_sem=sb_ss.at[d], recv_sem=sb_rs.at[d],
            device_id={"head": head ^ 1}, device_id_type=MESH,
        )
        net.start(sib[d])

    def chip_sum(d):
        own = share(((xi + d) % 4) * 2 + core)
        net.arrive(sib[d])
        return own + sib_recv[d].astype(F32)

    def to_chip(d):
        x_send[d] = chip_sum(d).astype(BF16)
        cp = pltpu.make_async_remote_copy(
            src_ref=x_send.at[d], dst_ref=x_recv.at[d], send_sem=x_ss.at[d], recv_sem=x_rs.at[d],
            device_id={"head": ((xi + d) % 4) * 2 + core}, device_id_type=MESH,
        )
        net.start(cp)
        xs.append((d, cp))

    to_sibling(2)
    to_sibling(1)
    to_chip(2)
    to_sibling(3)
    to_chip(1)
    to_sibling(0)
    to_chip(3)
    total = chip_sum(0)
    for d, cp in xs:
        net.arrive(cp)
        total = total + x_recv[d].astype(F32)

    fsend[...] = total.astype(BF16)
    fcopies = []
    for d in (3, 2, 1):
        cp = pltpu.make_async_remote_copy(
            src_ref=fsend.at[:, lane((yl + d) % 4)], dst_ref=fin.at[yl],
            send_sem=f_ss.at[d], recv_sem=f_rs.at[d],
            device_id={"ctx": base + (yl + d) % 4}, device_id_type=MESH,
        )
        net.start(cp)
        fcopies.append(cp)
    fin[yl] = fsend[:, lane(yl)]
    net.arrive(*fcopies)
    parts = [fin[j, 64 * m : 64 * m + 64, :] for m in range(2) for j in range(4)]
    out_ref[...] = jnp.concatenate(parts, axis=0).astype(F32).T.astype(BF16)

    net.finish()


def per_device(q, k, v, dec, beta, lw, w):
    vmem = pl.BlockSpec(memory_space=pltpu.VMEM)
    dma = pltpu.SemaphoreType.DMA
    return pl.pallas_call(
        kernel,
        out_shape=jax.ShapeDtypeStruct((TB, 512), BF16),
        in_specs=[pl.BlockSpec(memory_space=pltpu.HBM)] * 7,
        out_specs=vmem,
        scratch_shapes=[
            pltpu.VMEM((4, TB), F32),
            pltpu.VMEM((4, TB), F32),
            pltpu.VMEM((7, 4, TB), F32),
            pltpu.VMEM((4, 16, TB), F32),
            pltpu.VMEM((4, TB, DK), BF16),
            pltpu.VMEM((4, TB, DK), BF16),
            pltpu.VMEM((4, TB, DK), BF16),
            pltpu.VMEM((4, 16, TB), F32),
            pltpu.VMEM((4, TB, DK), F32),
            pltpu.VMEM((4, TB, TB), F32),
            pltpu.VMEM((4, TB, 2 * DK), F32),
            pltpu.VMEM((4, DK, 2 * DK), F32),
            pltpu.VMEM((4, TB, DK), F32),
            pltpu.VMEM((DK, 4 * TB), F32),
            pltpu.VMEM((DK, 4 * TB), F32),
            pltpu.VMEM((DK, 2 * DK), F32),
            pltpu.VMEM((DK, DK), F32),
            pltpu.VMEM((4, DK, 2 * DK), BF16),
            pltpu.VMEM((4, DK, 2 * DK), BF16),
            pltpu.VMEM((4 * DK, 4 * TB), BF16),
            pltpu.VMEM((8, 2, 64, 512), BF16),
            pltpu.VMEM((4, DK, 4 * TB), BF16),
            pltpu.VMEM((4, DK, 4 * TB), BF16),
            pltpu.VMEM((4, DK, 4 * TB), BF16),
            pltpu.VMEM((4, DK, 4 * TB), BF16),
            pltpu.VMEM((DK, 4 * TB), BF16),
            pltpu.VMEM((4, DK, TB), BF16),
            dma((3, 4)), dma((3, 4)), dma((4,)), dma((4,)), dma((4,)), dma((4,)),
            dma((4,)), dma((4,)), dma, dma, dma((2, 5)), dma((2, 5)),
            dma((4,)), dma((4,)), dma((4,)), dma((4,)), dma((4,)), dma((4,)), dma((7,)),
        ],
        compiler_params=pltpu.CompilerParams(
            collective_id=0, has_side_effects=True, vmem_limit_bytes=60 * 2**20
        ),
        name="mixer",
    )(q, k, v, dec.T, beta.T, lw.transpose(2, 1, 0), w.T)


def solution(mesh):
    spec = P("ctx", "head")
    return jax.shard_map(
        per_device,
        mesh=mesh,
        in_specs=(spec,) * 5 + (P("ctx", "head", None), P("head", "ctx")),
        out_specs=spec,
        check_vma=False,
    )
```

```python
import jax
import jax.numpy as jnp
from jax import lax
from jax.sharding import PartitionSpec as P
from jax.experimental import pallas as pl
from jax.experimental.pallas import tpu as pltpu

DK = 128
TB = 128
MESH = pl.DeviceIdType.MESH
F32 = jnp.float32
BF16 = jnp.bfloat16


def split(a):
    hi = a.astype(BF16)
    lo = (a - hi.astype(F32)).astype(BF16)
    return hi, lo


def dot3(a, b):
    ah, al = split(a)
    bh, bl = split(b)
    return jnp.dot(
        jnp.concatenate([ah, ah, al], axis=1),
        jnp.concatenate([bh, bl, bh], axis=0),
        preferred_element_type=F32,
    )


def dot3_nt(a, b):
    ah, al = split(a)
    bh, bl = split(b)
    return lax.dot_general(
        jnp.concatenate([ah, ah, al], axis=1),
        jnp.concatenate([bh, bl, bh], axis=1),
        (((1,), (1,)), ((), ())),
        preferred_element_type=F32,
    )


def unit_rows(x):
    return x * lax.rsqrt(jnp.sum(x * x, axis=-1, keepdims=True) + 1e-06)


class Copies:
    def __init__(self):
        self.sends = []
        self.arrivals = []

    def start(self, *copies):
        for cp in copies:
            cp.start()
            self.sends.append(cp)
            self.arrivals.append(cp)

    def arrive(self, *copies):
        for cp in copies:
            cp.wait_recv()
            self.arrivals = [c for c in self.arrivals if c is not cp]

    def finish(self):
        for cp in self.arrivals:
            cp.wait_recv()
        for cp in self.sends:
            cp.wait_send()


def kernel(
    q_hbm, k_hbm, v_hbm, dec_hbm, beta_hbm, lw_hbm, w_ref, out_ref,
    q_ref, k_ref, v_ref, dec_ref, beta_ref, lw_ref, small, rq, rk, rv, rs, kn, gm, wu, ab, cols, lrt, ot, tot, relay,
    st_send, st_recv, mt, wg, sib_send, sib_recv, x_send, x_recv, fsend, fin,
    kv_ss, kv_rs, st_ss, st_rs, o_ss, o_rs, w1_ss, w1_rs, w2_ss, w2_rs,
    sb_ss, sb_rs, x_ss, x_rs, f_ss, f_rs, in_s,
):
    net = Copies()
    ctx = lax.axis_index("ctx")
    head = lax.axis_index("head")
    zi = ctx // 8
    yi = ctx % 8
    yl = ctx % 4
    yh = yi // 4
    base = ctx - yl
    core = head % 2
    xi = head // 2

    def at_zy(z, y):
        return {"ctx": z * 8 + y}

    def lane(j):
        return pl.ds(pl.multiple_of(j * DK, DK), DK)

    barrier = pltpu.get_barrier_semaphore()
    for z in ((zi + 1) % 8, (zi + 7) % 8, zi ^ 2, zi ^ 4):
        pl.semaphore_signal(barrier, inc=1, device_id=at_zy(z, yi), device_id_type=MESH)
    pl.semaphore_signal(barrier, inc=1, device_id={"ctx": ctx ^ 4}, device_id_type=MESH)
    for d in range(1, 4):
        pl.semaphore_signal(
            barrier, inc=1, device_id={"ctx": base + (yl + d) % 4}, device_id_type=MESH
        )
    for d in (1, 3):
        pl.semaphore_signal(
            barrier, inc=1, device_id={"head": ((xi + d) % 4) * 2 + core}, device_id_type=MESH
        )
    pl.semaphore_signal(barrier, inc=1, device_id={"head": head ^ 1}, device_id_type=MESH)

    loads = [
        pltpu.make_async_copy(src, dst, in_s.at[i])
        for i, (src, dst) in enumerate(
            (
                (dec_hbm, dec_ref), (beta_hbm, beta_ref), (lw_hbm, lw_ref),
                (w_ref, wg.at[zi, yh]), (k_hbm, k_ref), (v_hbm, v_ref), (q_hbm, q_ref),
            )
        )
    ]
    for cp in loads:
        cp.start()

    for cp in loads[:3]:
        cp.wait()
    for j in range(4):
        small[j, 0:1, :] = dec_ref[j : j + 1]
        small[j, 1:2, :] = beta_ref[j : j + 1]
        for l in range(7):
            small[j, 2 + l : 3 + l, :] = lw_ref[l, j : j + 1]
        small[j, 9:16, :] = jnp.zeros((7, TB), F32)

    for cp in loads[3:]:
        cp.wait()
    pl.semaphore_wait(barrier, 11)

    def to_group(src, dst, a):
        copies = []
        for d in (3, 2, 1):
            to = (yl + d) % 4
            copies.append(
                pltpu.make_async_remote_copy(
                    src_ref=src.at[to] if a == 1 else src.at[:, lane(to)],
                    dst_ref=dst.at[yl], send_sem=kv_ss.at[a, d], recv_sem=kv_rs.at[a, d],
                    device_id={"ctx": base + to}, device_id_type=MESH,
                )
            )
        net.start(*copies)
        return copies

    k_copies = to_group(k_ref, rk, 0)
    s_copies = to_group(small, rs, 1)
    v_copies = to_group(v_ref, rv, 2)

    w_pair = pltpu.make_async_remote_copy(
        src_ref=wg.at[zi, yh], dst_ref=wg.at[zi, yh], send_sem=w1_ss, recv_sem=w1_rs,
        device_id={"ctx": ctx ^ 4}, device_id_type=MESH,
    )
    net.start(w_pair)

    def w_copy(sub, way, step):
        slot = (zi + (step - 1) * (2 * way - 1) + 8) % 8
        part = wg.at[slot, yh if sub == 0 else 1 - yh]
        if step == 4:
            part = part.at[pl.ds(32 * way, 32)]
        return pltpu.make_async_remote_copy(
            src_ref=part, dst_ref=part,
            send_sem=w2_ss.at[sub, way, step], recv_sem=w2_rs.at[sub, way, step],
            device_id=at_zy((zi + 1 + 6 * way) % 8, yi), device_id_type=MESH,
        )

    w_ring = [
        [[w_copy(sub, way, step) for way in range(2)] for step in range(1, 5)] for sub in range(2)
    ]

    def w_pass_on(sub, step):
        net.arrive(*w_ring[sub][step - 1])
        net.start(*w_ring[sub][step])

    net.start(*w_ring[0][0])

    rs[yl] = small[yl]
    rk[yl] = k_ref[:, lane(yl)]
    rv[yl] = v_ref[:, lane(yl)]
    rq[yl] = q_ref[:, lane(yl)]

    ri = lax.broadcasted_iota(jnp.int32, (TB, TB), 0)
    ci = lax.broadcasted_iota(jnp.int32, (TB, TB), 1)
    eye = (ri == ci).astype(F32)
    upto = (ri <= ci).astype(F32)

    def pairs(slots, values_here=None):
        n = len(slots)
        ls, keys, betas, tails, lasts = [], [], [], [], []
        for s in slots:
            sm = rs[s]
            g_rows = -jnp.dot(
                sm, upto, preferred_element_type=F32, precision=lax.Precision.HIGHEST
            )
            g_row = g_rows[0:1]
            col = jnp.concatenate([g_row, sm[1:8]], axis=0)
            col = jnp.concatenate([col, jnp.zeros((TB - 8, TB), F32)], axis=0).T
            g_col = col[:, 0:1]
            b_col = col[:, 1:2]
            growth = jnp.exp(g_col)
            g_last = g_row[:, TB - 1 : TB]
            ratio = jnp.where(ci <= ri, jnp.exp(jnp.minimum(g_col - g_row, 0.0)), 0.0)
            kk = unit_rows(rk[s].astype(F32))
            kn[s] = kk
            gm[s] = ratio
            cols[s] = jnp.broadcast_to(growth, (TB, DK))
            ls.append(jnp.where(ci < ri, b_col * ratio * dot3_nt(kk, kk), 0.0))
            keys.append((b_col * growth) * kk)
            betas.append(b_col)
            tails.append(jnp.exp(g_last - g_col) * kk)
            lasts.append(jnp.exp(g_last))
        inv = [eye - jnp.where((ri % 2 == 1) & (ci == ri - 1), l, 0.0) for l in ls]
        b = 2
        while b < TB:
            mask = ((ri // b) % 2 == 1) & (ci // b == ri // b - 1)
            mid = [dot3(inv[i], jnp.where(mask, ls[i], 0.0)) for i in range(n)]
            inv = [inv[i] - dot3(mid[i], inv[i]) for i in range(n)]
            b *= 2
        if values_here is not None:
            values_here()
        sol = [
            dot3(
                inv[i],
                jnp.concatenate([keys[i], betas[i] * rv[s].astype(F32)], axis=1),
            )
            for i, s in enumerate(slots)
        ]
        for i, s in enumerate(slots):
            wu[s] = sol[i]
            m = dot3(tails[i].T, sol[i])
            ab[s, :, 0:DK] = lasts[i] * eye - m[:, 0:DK]
            ab[s, :, DK:] = m[:, DK:]

    pairs([yl])
    w_pass_on(0, 1)
    net.arrive(w_pair)
    net.start(*w_ring[1][0])

    net.arrive(*s_copies)
    net.arrive(*k_copies)
    q_copies = to_group(q_ref, rq, 3)
    w_pass_on(0, 2)

    pairs([(yl + d) % 4 for d in range(1, 4)], lambda: net.arrive(*v_copies))

    def apply(second, first):
        r = dot3(second[:, 0:DK], first)
        return jnp.concatenate([r[:, 0:DK], r[:, DK:] + second[:, DK:]], axis=1)

    ab01 = apply(ab[1], ab[0])
    ab23 = apply(ab[3], ab[2])
    group = apply(ab23, ab01)

    def level_copy(i):
        if i < 3:
            src, dst = st_send.at[i], st_recv.at[i]
        else:
            src, dst = st_send.at[i, :, pl.ds(DK, DK)], st_recv.at[i, :, pl.ds(DK, DK)]
        return pltpu.make_async_remote_copy(
            src_ref=src, dst_ref=dst, send_sem=st_ss.at[i], recv_sem=st_rs.at[i],
            device_id={"ctx": ctx ^ (4 << i)}, device_id_type=MESH,
        )

    levels = [level_copy(i) for i in range(4)]
    tot[...] = group
    st_send[0] = group.astype(BF16)
    net.start(levels[0])
    relay[...] = eye
    w_pass_on(1, 1)
    w_pass_on(0, 3)

    net.arrive(*q_copies)
    b01 = ab01[:, DK:]
    a2 = ab[2, :, 0:DK]
    r3 = dot3(a2, ab01)
    starts = [None, ab[0, :, 0:DK], ab01[:, 0:DK], r3[:, 0:DK]]
    for s in range(4):
        kk = kn[s]
        qq = unit_rows(rq[s].astype(F32))
        p = dot3_nt(qq, kk) * gm[s]
        pwu = dot3(p, wu[s])
        moved = cols[s] * qq - pwu[:, 0:DK]
        inner = pwu[:, DK:]
        wt = rs[s]
        o = wt[2:3] * inner.T
        if s == 0:
            lifted = moved
        elif s == 1:
            r = dot3(moved, ab[0])
            lifted = r[:, 0:DK]
            o = o + wt[3:4] * r[:, DK:].T
        elif s == 2:
            r = dot3(moved, ab01)
            lifted = r[:, 0:DK]
            o = o + wt[4:5] * r[:, DK:].T
        else:
            r = dot3(moved, jnp.concatenate([r3, ab[2, :, DK:]], axis=1))
            lifted = r[:, 0:DK]
            o = o + wt[4:5] * r[:, DK : 2 * DK].T + wt[3:4] * r[:, 2 * DK :].T
        lrt[:, s * TB : (s + 1) * TB] = lifted.T
        ot[:, s * TB : (s + 1) * TB] = o

    def add_level(i, state):
        t = dot3(state.T, lrt[...])
        for s in range(4):
            sl = slice(s * TB, (s + 1) * TB)
            ot[:, sl] = ot[:, sl] + rs[s, 4 + i + 1 : 4 + i + 2, :] * t[:, sl]

    w_pass_on(1, 2)

    for i in range(4):
        upper = (ctx // (4 << i)) % 2 == 1
        if i < 3:
            net.arrive(levels[i])
            other = st_recv[i].astype(F32)
            own = tot[...]
            first = jnp.where(upper, other, own)
            second = jnp.where(upper, own, other)
            old = relay[...]
            r = dot3(jnp.concatenate([second[:, 0:DK], old], axis=0), first)
            new_b = r[0:DK, DK:] + second[:, DK:]
            tot[:, 0:DK] = r[0:DK, 0:DK]
            tot[:, DK:] = new_b
            st_send[i + 1, :, 0:DK] = r[0:DK, 0:DK].astype(BF16)
            st_send[i + 1, :, DK:] = new_b.astype(BF16)
            if i < 2:
                net.start(levels[i + 1])
            else:
                @pl.when((ctx // 32) % 2 == 0)
                def _():
                    levels[3].start()
            relay[...] = jnp.where(upper, r[DK:, 0:DK], old)

            @pl.when(upper)
            def _():
                add_level(i, r[DK:, DK:])

            if i == 0:
                w_pass_on(1, 3)
        else:
            @pl.when(upper)
            def _():
                levels[3].wait_recv()
                add_level(3, dot3(relay[...], st_recv[3, :, DK:].astype(F32)))

            @pl.when(jnp.logical_not(upper))
            def _():
                levels[3].wait_send()

    mine = mt.at[pl.ds(pl.multiple_of(yl * DK, DK), DK)]
    mine[...] = ot[...].astype(BF16)
    o_copies = []
    for d in (3, 2, 1):
        cp = pltpu.make_async_remote_copy(
            src_ref=mine, dst_ref=mine, send_sem=o_ss.at[d], recv_sem=o_rs.at[d],
            device_id={"ctx": base + (yl + d) % 4}, device_id_type=MESH,
        )
        net.start(cp)
        o_copies.append(cp)
    net.arrive(*w_ring[0][3])
    net.arrive(*w_ring[1][3])
    net.arrive(*o_copies)

    def share(block):
        w = wg[block].reshape(128, 512)
        return jnp.dot(w, mt[...], preferred_element_type=F32)

    sib, xs = {}, []

    def to_sibling(d):
        sib_send[d] = share(((xi + d) % 4) * 2 + 1 - core).astype(BF16)
        sib[d] = pltpu.make_async_remote_copy(
            src_ref=sib_send.at[d], dst_ref=sib_recv.at[d], send_sem=sb_ss.at[d], recv_sem=sb_rs.at[d],
            device_id={"head": head ^ 1}, device_id_type=MESH,
        )
        net.start(sib[d])

    def chip_sum(d):
        own = share(((xi + d) % 4) * 2 + core)
        net.arrive(sib[d])
        return own + sib_recv[d].astype(F32)

    def x_copy(i, src, way):
        return pltpu.make_async_remote_copy(
            src_ref=src, dst_ref=x_recv.at[i], send_sem=x_ss.at[i], recv_sem=x_rs.at[i],
            device_id={"head": ((xi + 1 + 2 * way) % 4) * 2 + core}, device_id_type=MESH,
        )

    halves = (pl.ds(0, 64), pl.ds(64, 64))
    x_far = [x_copy(way, x_send.at[2, halves[way]], way) for way in range(2)]
    x_plain = [x_copy(2 + way, x_send.at[1 + 2 * way, halves[1 - way]], way) for way in range(2)]
    x_added = [x_copy(4 + way, x_send.at[1 + 2 * way, halves[way]], way) for way in range(2)]

    def to_neighbour(way):
        near = chip_sum(1 + 2 * way)
        keep, add = (near[64:], near[:64]) if way == 0 else (near[:64], near[64:])
        x_send[1 + 2 * way, halves[1 - way], :] = keep.astype(BF16)
        net.start(x_plain[way])
        return add

    def pass_added(way, add):
        net.arrive(x_far[way])
        x_send[1 + 2 * way, halves[way], :] = (add + x_recv[way].astype(F32)).astype(BF16)
        net.start(x_added[way])

    to_sibling(2)
    to_sibling(1)
    x_send[2] = chip_sum(2).astype(BF16)
    net.start(*x_far)
    to_sibling(3)
    add0 = to_neighbour(0)
    to_sibling(0)
    add1 = to_neighbour(1)
    pass_added(0, add0)
    pass_added(1, add1)
    total = chip_sum(0)
    net.arrive(*x_plain, *x_added)
    low = x_recv[3].astype(F32) + x_recv[4].astype(F32)
    high = x_recv[2].astype(F32) + x_recv[5].astype(F32)
    total = total + jnp.concatenate([low, high], axis=0)

    fsend[...] = total.astype(BF16)
    fcopies = []
    for d in (3, 2, 1):
        cp = pltpu.make_async_remote_copy(
            src_ref=fsend.at[:, lane((yl + d) % 4)], dst_ref=fin.at[yl],
            send_sem=f_ss.at[d], recv_sem=f_rs.at[d],
            device_id={"ctx": base + (yl + d) % 4}, device_id_type=MESH,
        )
        net.start(cp)
        fcopies.append(cp)
    fin[yl] = fsend[:, lane(yl)]
    net.arrive(*fcopies)
    parts = [fin[j, 64 * m : 64 * m + 64, :] for m in range(2) for j in range(4)]
    out_ref[...] = jnp.concatenate(parts, axis=0).astype(F32).T.astype(BF16)

    net.finish()


def per_device(q, k, v, dec, beta, lw, w):
    vmem = pl.BlockSpec(memory_space=pltpu.VMEM)
    dma = pltpu.SemaphoreType.DMA
    return pl.pallas_call(
        kernel,
        out_shape=jax.ShapeDtypeStruct((TB, 512), BF16),
        in_specs=[pl.BlockSpec(memory_space=pltpu.HBM)] * 7,
        out_specs=vmem,
        scratch_shapes=[
            pltpu.VMEM((TB, 4 * DK), BF16),
            pltpu.VMEM((TB, 4 * DK), BF16),
            pltpu.VMEM((TB, 4 * DK), BF16),
            pltpu.VMEM((4, TB), F32),
            pltpu.VMEM((4, TB), F32),
            pltpu.VMEM((7, 4, TB), F32),
            pltpu.VMEM((4, 16, TB), F32),
            pltpu.VMEM((4, TB, DK), BF16),
            pltpu.VMEM((4, TB, DK), BF16),
            pltpu.VMEM((4, TB, DK), BF16),
            pltpu.VMEM((4, 16, TB), F32),
            pltpu.VMEM((4, TB, DK), F32),
            pltpu.VMEM((4, TB, TB), F32),
            pltpu.VMEM((4, TB, 2 * DK), F32),
            pltpu.VMEM((4, DK, 2 * DK), F32),
            pltpu.VMEM((4, TB, DK), F32),
            pltpu.VMEM((DK, 4 * TB), F32),
            pltpu.VMEM((DK, 4 * TB), F32),
            pltpu.VMEM((DK, 2 * DK), F32),
            pltpu.VMEM((DK, DK), F32),
            pltpu.VMEM((4, DK, 2 * DK), BF16),
            pltpu.VMEM((4, DK, 2 * DK), BF16),
            pltpu.VMEM((4 * DK, 4 * TB), BF16),
            pltpu.VMEM((8, 2, 64, 512), BF16),
            pltpu.VMEM((4, DK, 4 * TB), BF16),
            pltpu.VMEM((4, DK, 4 * TB), BF16),
            pltpu.VMEM((4, DK, 4 * TB), BF16),
            pltpu.VMEM((6, 64, 4 * TB), BF16),
            pltpu.VMEM((DK, 4 * TB), BF16),
            pltpu.VMEM((4, DK, TB), BF16),
            dma((4, 4)), dma((4, 4)), dma((4,)), dma((4,)),
            dma((4,)), dma((4,)), dma, dma, dma((2, 2, 5)), dma((2, 2, 5)),
            dma((4,)), dma((4,)), dma((6,)), dma((6,)), dma((4,)), dma((4,)), dma((7,)),
        ],
        compiler_params=pltpu.CompilerParams(
            collective_id=0, has_side_effects=True, vmem_limit_bytes=60 * 2**20
        ),
        name="mixer",
    )(q, k, v, dec.T, beta.T, lw.transpose(2, 1, 0), w.T)


def solution(mesh):
    spec = P("ctx", "head")
    return jax.shard_map(
        per_device,
        mesh=mesh,
        in_specs=(spec,) * 5 + (P("ctx", "head", None), P("head", "ctx")),
        out_specs=spec,
        check_vma=False,
    )
```

```python
import jax
import jax.numpy as jnp
from jax import lax
from jax.sharding import PartitionSpec as P
from jax.experimental import pallas as pl
from jax.experimental.pallas import tpu as pltpu

DK = 128
TB = 128
MESH = pl.DeviceIdType.MESH
F32 = jnp.float32
BF16 = jnp.bfloat16


def split(a):
    hi = a.astype(BF16)
    lo = (a - hi.astype(F32)).astype(BF16)
    return hi, lo


def dot3(a, b):
    ah, al = split(a)
    bh, bl = split(b)
    return jnp.dot(
        jnp.concatenate([ah, ah, al], axis=1),
        jnp.concatenate([bh, bl, bh], axis=0),
        preferred_element_type=F32,
    )


def dot3_nt(a, b):
    ah, al = split(a)
    bh, bl = split(b)
    return lax.dot_general(
        jnp.concatenate([ah, ah, al], axis=1),
        jnp.concatenate([bh, bl, bh], axis=1),
        (((1,), (1,)), ((), ())),
        preferred_element_type=F32,
    )


def unit_rows(x):
    return x * lax.rsqrt(jnp.sum(x * x, axis=-1, keepdims=True) + 1e-06)


class Copies:
    def __init__(self):
        self.sends = []
        self.arrivals = []

    def start(self, *copies):
        for cp in copies:
            cp.start()
            self.sends.append(cp)
            self.arrivals.append(cp)

    def arrive(self, *copies):
        for cp in copies:
            cp.wait_recv()
            self.arrivals = [c for c in self.arrivals if c is not cp]

    def finish(self):
        for cp in self.arrivals:
            cp.wait_recv()
        for cp in self.sends:
            cp.wait_send()


def kernel(
    q_hbm, k_hbm, v_hbm, dec_hbm, beta_hbm, lw_hbm, w_ref, out_ref,
    q_ref, k_ref, v_ref, dec_ref, beta_ref, lw_ref, small, rq, rk, rv, rs, kn, gm, wu, ab, cols, lrt, ot, tot, relay,
    st_send, st_recv, mt, wg, sib_send, sib_recv, x_send, x_recv, fsend, fin,
    kv_ss, kv_rs, st_ss, st_rs, o_ss, o_rs, w1_ss, w1_rs, w2_ss, w2_rs,
    sb_ss, sb_rs, x_ss, x_rs, f_ss, f_rs, in_s,
):
    net = Copies()
    ctx = lax.axis_index("ctx")
    head = lax.axis_index("head")
    zi = ctx // 8
    yi = ctx % 8
    yl = ctx % 4
    yh = yi // 4
    base = ctx - yl
    core = head % 2
    xi = head // 2

    def at_zy(z, y):
        return {"ctx": z * 8 + y}

    def lane(j):
        return pl.ds(pl.multiple_of(j * DK, DK), DK)

    barrier = pltpu.get_barrier_semaphore()
    for z in ((zi + 1) % 8, (zi + 7) % 8, zi ^ 2, zi ^ 4):
        pl.semaphore_signal(barrier, inc=1, device_id=at_zy(z, yi), device_id_type=MESH)
    pl.semaphore_signal(barrier, inc=1, device_id={"ctx": ctx ^ 4}, device_id_type=MESH)
    for d in range(1, 4):
        pl.semaphore_signal(
            barrier, inc=1, device_id={"ctx": base + (yl + d) % 4}, device_id_type=MESH
        )
    for d in (1, 3):
        pl.semaphore_signal(
            barrier, inc=1, device_id={"head": ((xi + d) % 4) * 2 + core}, device_id_type=MESH
        )
    pl.semaphore_signal(barrier, inc=1, device_id={"head": head ^ 1}, device_id_type=MESH)

    loads = [
        pltpu.make_async_copy(src, dst, in_s.at[i])
        for i, (src, dst) in enumerate(
            (
                (dec_hbm, dec_ref), (beta_hbm, beta_ref), (lw_hbm, lw_ref),
                (w_ref, wg.at[zi, yh]), (k_hbm, k_ref), (v_hbm, v_ref), (q_hbm, q_ref),
            )
        )
    ]
    for cp in loads:
        cp.start()

    for cp in loads[:3]:
        cp.wait()
    for j in range(4):
        small[j, 0:1, :] = dec_ref[j : j + 1]
        small[j, 1:2, :] = beta_ref[j : j + 1]
        for l in range(7):
            small[j, 2 + l : 3 + l, :] = lw_ref[l, j : j + 1]
        small[j, 9:16, :] = jnp.zeros((7, TB), F32)

    for cp in loads[3:]:
        cp.wait()
    pl.semaphore_wait(barrier, 11)

    def to_group(src, dst, a):
        copies = []
        for d in (3, 2, 1):
            to = (yl + d) % 4
            copies.append(
                pltpu.make_async_remote_copy(
                    src_ref=src.at[to] if a == 1 else src.at[:, lane(to)],
                    dst_ref=dst.at[yl], send_sem=kv_ss.at[a, d], recv_sem=kv_rs.at[a, d],
                    device_id={"ctx": base + to}, device_id_type=MESH,
                )
            )
        net.start(*copies)
        return copies

    k_copies = to_group(k_ref, rk, 0)
    s_copies = to_group(small, rs, 1)
    v_copies = to_group(v_ref, rv, 2)

    w_pair = pltpu.make_async_remote_copy(
        src_ref=wg.at[zi, yh], dst_ref=wg.at[zi, yh], send_sem=w1_ss, recv_sem=w1_rs,
        device_id={"ctx": ctx ^ 4}, device_id_type=MESH,
    )
    net.start(w_pair)

    def w_copy(sub, way, step):
        slot = (zi + (step - 1) * (2 * way - 1) + 8) % 8
        part = wg.at[slot, yh if sub == 0 else 1 - yh]
        if step == 4:
            part = part.at[pl.ds(32 * way, 32)]
        return pltpu.make_async_remote_copy(
            src_ref=part, dst_ref=part,
            send_sem=w2_ss.at[sub, way, step], recv_sem=w2_rs.at[sub, way, step],
            device_id=at_zy((zi + 1 + 6 * way) % 8, yi), device_id_type=MESH,
        )

    w_ring = [
        [[w_copy(sub, way, step) for way in range(2)] for step in range(1, 5)] for sub in range(2)
    ]

    def w_pass_on(sub, step):
        net.arrive(*w_ring[sub][step - 1])
        net.start(*w_ring[sub][step])

    net.start(*w_ring[0][0])

    rs[yl] = small[yl]
    rk[yl] = k_ref[:, lane(yl)]
    rv[yl] = v_ref[:, lane(yl)]
    rq[yl] = q_ref[:, lane(yl)]

    ri = lax.broadcasted_iota(jnp.int32, (TB, TB), 0)
    ci = lax.broadcasted_iota(jnp.int32, (TB, TB), 1)
    eye = (ri == ci).astype(F32)
    upto = (ri <= ci).astype(F32)

    def pairs(slots, values_here=None):
        n = len(slots)
        ls, keys, betas, tails, lasts = [], [], [], [], []
        for s in slots:
            sm = rs[s]
            g_rows = -jnp.dot(
                sm, upto, preferred_element_type=F32, precision=lax.Precision.HIGHEST
            )
            g_row = g_rows[0:1]
            col = jnp.concatenate([g_row, sm[1:8]], axis=0)
            col = jnp.concatenate([col, jnp.zeros((TB - 8, TB), F32)], axis=0).T
            g_col = col[:, 0:1]
            b_col = col[:, 1:2]
            growth = jnp.exp(g_col)
            g_last = g_row[:, TB - 1 : TB]
            ratio = jnp.where(ci <= ri, jnp.exp(jnp.minimum(g_col - g_row, 0.0)), 0.0)
            kk = unit_rows(rk[s].astype(F32))
            kn[s] = kk
            gm[s] = ratio
            cols[s] = jnp.broadcast_to(growth, (TB, DK))
            ls.append(jnp.where(ci < ri, b_col * ratio * dot3_nt(kk, kk), 0.0))
            keys.append((b_col * growth) * kk)
            betas.append(b_col)
            tails.append(jnp.exp(g_last - g_col) * kk)
            lasts.append(jnp.exp(g_last))
        inv = [eye - jnp.where((ri % 2 == 1) & (ci == ri - 1), l, 0.0) for l in ls]
        b = 2
        while b < TB:
            mask = ((ri // b) % 2 == 1) & (ci // b == ri // b - 1)
            mid = [dot3(inv[i], jnp.where(mask, ls[i], 0.0)) for i in range(n)]
            inv = [inv[i] - dot3(mid[i], inv[i]) for i in range(n)]
            b *= 2
        if values_here is not None:
            values_here()
        sol = [
            dot3(
                inv[i],
                jnp.concatenate([keys[i], betas[i] * rv[s].astype(F32)], axis=1),
            )
            for i, s in enumerate(slots)
        ]
        for i, s in enumerate(slots):
            wu[s] = sol[i]
            m = dot3(tails[i].T, sol[i])
            ab[s, :, 0:DK] = lasts[i] * eye - m[:, 0:DK]
            ab[s, :, DK:] = m[:, DK:]

    pairs([yl])
    w_pass_on(0, 1)

    net.arrive(*s_copies)
    net.arrive(*k_copies)
    q_copies = to_group(q_ref, rq, 3)
    w_pass_on(0, 2)

    def values_here():
        net.arrive(*v_copies)
        net.arrive(w_pair)
        net.start(*w_ring[1][0])

    pairs([(yl + d) % 4 for d in range(1, 4)], values_here)

    def apply(second, first):
        r = dot3(second[:, 0:DK], first)
        return jnp.concatenate([r[:, 0:DK], r[:, DK:] + second[:, DK:]], axis=1)

    ab01 = apply(ab[1], ab[0])
    ab23 = apply(ab[3], ab[2])
    group = apply(ab23, ab01)

    def level_copy(i):
        if i < 3:
            src, dst = st_send.at[i], st_recv.at[i]
        else:
            src, dst = st_send.at[i, :, pl.ds(DK, DK)], st_recv.at[i, :, pl.ds(DK, DK)]
        return pltpu.make_async_remote_copy(
            src_ref=src, dst_ref=dst, send_sem=st_ss.at[i], recv_sem=st_rs.at[i],
            device_id={"ctx": ctx ^ (4 << i)}, device_id_type=MESH,
        )

    levels = [level_copy(i) for i in range(4)]
    tot[...] = group
    st_send[0] = group.astype(BF16)
    net.start(levels[0])
    relay[...] = eye
    w_pass_on(1, 1)
    w_pass_on(0, 3)

    net.arrive(*q_copies)
    b01 = ab01[:, DK:]
    a2 = ab[2, :, 0:DK]
    r3 = dot3(a2, ab01)
    starts = [None, ab[0, :, 0:DK], ab01[:, 0:DK], r3[:, 0:DK]]
    for s in range(4):
        kk = kn[s]
        qq = unit_rows(rq[s].astype(F32))
        p = dot3_nt(qq, kk) * gm[s]
        pwu = dot3(p, wu[s])
        moved = cols[s] * qq - pwu[:, 0:DK]
        inner = pwu[:, DK:]
        wt = rs[s]
        o = wt[2:3] * inner.T
        if s == 0:
            lifted = moved
        elif s == 1:
            r = dot3(moved, ab[0])
            lifted = r[:, 0:DK]
            o = o + wt[3:4] * r[:, DK:].T
        elif s == 2:
            r = dot3(moved, ab01)
            lifted = r[:, 0:DK]
            o = o + wt[4:5] * r[:, DK:].T
        else:
            r = dot3(moved, jnp.concatenate([r3, ab[2, :, DK:]], axis=1))
            lifted = r[:, 0:DK]
            o = o + wt[4:5] * r[:, DK : 2 * DK].T + wt[3:4] * r[:, 2 * DK :].T
        lrt[:, s * TB : (s + 1) * TB] = lifted.T
        ot[:, s * TB : (s + 1) * TB] = o

    def add_level(i, state, lifted=None):
        t = dot3(state.T, lrt[...] if lifted is None else lifted)
        for s in range(4):
            sl = slice(s * TB, (s + 1) * TB)
            ot[:, sl] = ot[:, sl] + rs[s, 4 + i + 1 : 4 + i + 2, :] * t[:, sl]

    for i in range(4):
        upper = (ctx // (4 << i)) % 2 == 1
        if i < 3:
            net.arrive(levels[i])
            other = st_recv[i].astype(F32)
            own = tot[...]
            first = jnp.where(upper, other, own)
            second = jnp.where(upper, own, other)
            old = relay[...]
            r = dot3(jnp.concatenate([second[:, 0:DK], old], axis=0), first)
            new_b = r[0:DK, DK:] + second[:, DK:]
            tot[:, 0:DK] = r[0:DK, 0:DK]
            tot[:, DK:] = new_b
            st_send[i + 1, :, 0:DK] = r[0:DK, 0:DK].astype(BF16)
            st_send[i + 1, :, DK:] = new_b.astype(BF16)
            if i < 2:
                net.start(levels[i + 1])
            else:
                @pl.when((ctx // 32) % 2 == 0)
                def _():
                    levels[3].start()
            relay[...] = jnp.where(upper, r[DK:, 0:DK], old)

            @pl.when(upper)
            def _():
                add_level(i, r[DK:, DK:])

            if i < 2:
                w_pass_on(1, 2 + i)
        else:
            @pl.when(upper)
            def _():
                lifted = dot3(relay[...].T, lrt[...])
                levels[3].wait_recv()
                add_level(3, st_recv[3, :, DK:].astype(F32), lifted)

            @pl.when(jnp.logical_not(upper))
            def _():
                levels[3].wait_send()

    mine = mt.at[pl.ds(pl.multiple_of(yl * DK, DK), DK)]
    mine[...] = ot[...].astype(BF16)
    o_copies = []
    for d in (3, 2, 1):
        cp = pltpu.make_async_remote_copy(
            src_ref=mine, dst_ref=mine, send_sem=o_ss.at[d], recv_sem=o_rs.at[d],
            device_id={"ctx": base + (yl + d) % 4}, device_id_type=MESH,
        )
        net.start(cp)
        o_copies.append(cp)
    net.arrive(*w_ring[0][3])
    net.arrive(*w_ring[1][3])
    net.arrive(*o_copies)

    def share(block):
        w = wg[block].reshape(128, 512)
        return jnp.dot(w, mt[...], preferred_element_type=F32)

    sib, xs = {}, []

    def to_sibling(d):
        sib_send[d] = share(((xi + d) % 4) * 2 + 1 - core).astype(BF16)
        sib[d] = pltpu.make_async_remote_copy(
            src_ref=sib_send.at[d], dst_ref=sib_recv.at[d], send_sem=sb_ss.at[d], recv_sem=sb_rs.at[d],
            device_id={"head": head ^ 1}, device_id_type=MESH,
        )
        net.start(sib[d])

    def chip_sum(d):
        own = share(((xi + d) % 4) * 2 + core)
        net.arrive(sib[d])
        return own + sib_recv[d].astype(F32)

    def x_copy(i, src, way):
        return pltpu.make_async_remote_copy(
            src_ref=src, dst_ref=x_recv.at[i], send_sem=x_ss.at[i], recv_sem=x_rs.at[i],
            device_id={"head": ((xi + 1 + 2 * way) % 4) * 2 + core}, device_id_type=MESH,
        )

    halves = (pl.ds(0, 64), pl.ds(64, 64))
    x_far = [x_copy(way, x_send.at[2, halves[way]], way) for way in range(2)]
    x_plain = [x_copy(2 + way, x_send.at[1 + 2 * way, halves[1 - way]], way) for way in range(2)]
    x_added = [x_copy(4 + way, x_send.at[1 + 2 * way, halves[way]], way) for way in range(2)]

    def to_neighbour(way):
        near = chip_sum(1 + 2 * way)
        keep, add = (near[64:], near[:64]) if way == 0 else (near[:64], near[64:])
        x_send[1 + 2 * way, halves[1 - way], :] = keep.astype(BF16)
        net.start(x_plain[way])
        return add

    def pass_added(way, add):
        net.arrive(x_far[way])
        x_send[1 + 2 * way, halves[way], :] = (add + x_recv[way].astype(F32)).astype(BF16)
        net.start(x_added[way])

    for d in (2, 1, 3, 0):
        to_sibling(d)
    x_send[2] = chip_sum(2).astype(BF16)
    net.start(*x_far)
    add0 = to_neighbour(0)
    add1 = to_neighbour(1)
    pass_added(0, add0)
    pass_added(1, add1)
    total = chip_sum(0)
    net.arrive(*x_plain, *x_added)
    low = x_recv[3].astype(F32) + x_recv[4].astype(F32)
    high = x_recv[2].astype(F32) + x_recv[5].astype(F32)
    total = total + jnp.concatenate([low, high], axis=0)

    fsend[...] = total.astype(BF16)
    fcopies = []
    for d in (3, 2, 1):
        cp = pltpu.make_async_remote_copy(
            src_ref=fsend.at[:, lane((yl + d) % 4)], dst_ref=fin.at[yl],
            send_sem=f_ss.at[d], recv_sem=f_rs.at[d],
            device_id={"ctx": base + (yl + d) % 4}, device_id_type=MESH,
        )
        net.start(cp)
        fcopies.append(cp)
    fin[yl] = fsend[:, lane(yl)]
    net.arrive(*fcopies)
    parts = [fin[j, 64 * m : 64 * m + 64, :] for m in range(2) for j in range(4)]
    out_ref[...] = jnp.concatenate(parts, axis=0).astype(F32).T.astype(BF16)

    net.finish()


def per_device(q, k, v, dec, beta, lw, w):
    vmem = pl.BlockSpec(memory_space=pltpu.VMEM)
    dma = pltpu.SemaphoreType.DMA
    return pl.pallas_call(
        kernel,
        out_shape=jax.ShapeDtypeStruct((TB, 512), BF16),
        in_specs=[pl.BlockSpec(memory_space=pltpu.HBM)] * 7,
        out_specs=vmem,
        scratch_shapes=[
            pltpu.VMEM((TB, 4 * DK), BF16),
            pltpu.VMEM((TB, 4 * DK), BF16),
            pltpu.VMEM((TB, 4 * DK), BF16),
            pltpu.VMEM((4, TB), F32),
            pltpu.VMEM((4, TB), F32),
            pltpu.VMEM((7, 4, TB), F32),
            pltpu.VMEM((4, 16, TB), F32),
            pltpu.VMEM((4, TB, DK), BF16),
            pltpu.VMEM((4, TB, DK), BF16),
            pltpu.VMEM((4, TB, DK), BF16),
            pltpu.VMEM((4, 16, TB), F32),
            pltpu.VMEM((4, TB, DK), F32),
            pltpu.VMEM((4, TB, TB), F32),
            pltpu.VMEM((4, TB, 2 * DK), F32),
            pltpu.VMEM((4, DK, 2 * DK), F32),
            pltpu.VMEM((4, TB, DK), F32),
            pltpu.VMEM((DK, 4 * TB), F32),
            pltpu.VMEM((DK, 4 * TB), F32),
            pltpu.VMEM((DK, 2 * DK), F32),
            pltpu.VMEM((DK, DK), F32),
            pltpu.VMEM((4, DK, 2 * DK), BF16),
            pltpu.VMEM((4, DK, 2 * DK), BF16),
            pltpu.VMEM((4 * DK, 4 * TB), BF16),
            pltpu.VMEM((8, 2, 64, 512), BF16),
            pltpu.VMEM((4, DK, 4 * TB), BF16),
            pltpu.VMEM((4, DK, 4 * TB), BF16),
            pltpu.VMEM((4, DK, 4 * TB), BF16),
            pltpu.VMEM((6, 64, 4 * TB), BF16),
            pltpu.VMEM((DK, 4 * TB), BF16),
            pltpu.VMEM((4, DK, TB), BF16),
            dma((4, 4)), dma((4, 4)), dma((4,)), dma((4,)),
            dma((4,)), dma((4,)), dma, dma, dma((2, 2, 5)), dma((2, 2, 5)),
            dma((4,)), dma((4,)), dma((6,)), dma((6,)), dma((4,)), dma((4,)), dma((7,)),
        ],
        compiler_params=pltpu.CompilerParams(
            collective_id=0, has_side_effects=True, vmem_limit_bytes=60 * 2**20
        ),
        name="mixer",
    )(q, k, v, dec.T, beta.T, lw.transpose(2, 1, 0), w.T)


def solution(mesh):
    spec = P("ctx", "head")
    return jax.shard_map(
        per_device,
        mesh=mesh,
        in_specs=(spec,) * 5 + (P("ctx", "head", None), P("head", "ctx")),
        out_specs=spec,
        check_vma=False,
    )
```

```python
import jax
import jax.numpy as jnp
from jax import lax
from jax.sharding import PartitionSpec as P
from jax.experimental import pallas as pl
from jax.experimental.pallas import tpu as pltpu

DK = 128
TB = 128
MESH = pl.DeviceIdType.MESH
F32 = jnp.float32
BF16 = jnp.bfloat16


def split(a):
    hi = a.astype(BF16)
    lo = (a - hi.astype(F32)).astype(BF16)
    return hi, lo


def dot3(a, b):
    ah, al = split(a)
    bh, bl = split(b)
    return jnp.dot(
        jnp.concatenate([ah, ah, al], axis=1),
        jnp.concatenate([bh, bl, bh], axis=0),
        preferred_element_type=F32,
    )


def dot3_nt(a, b):
    ah, al = split(a)
    bh, bl = split(b)
    return lax.dot_general(
        jnp.concatenate([ah, ah, al], axis=1),
        jnp.concatenate([bh, bl, bh], axis=1),
        (((1,), (1,)), ((), ())),
        preferred_element_type=F32,
    )


def unit_rows(x):
    return x * lax.rsqrt(jnp.sum(x * x, axis=-1, keepdims=True) + 1e-06)


class Copies:
    def __init__(self):
        self.sends = []
        self.arrivals = []

    def start(self, *copies):
        for cp in copies:
            cp.start()
            self.sends.append(cp)
            self.arrivals.append(cp)

    def arrive(self, *copies):
        for cp in copies:
            cp.wait_recv()
            self.arrivals = [c for c in self.arrivals if c is not cp]

    def finish(self):
        for cp in self.arrivals:
            cp.wait_recv()
        for cp in self.sends:
            cp.wait_send()


def kernel(
    q_hbm, k_hbm, v_hbm, dec_hbm, beta_hbm, lw_hbm, w_ref, out_ref,
    q_ref, k_ref, v_ref, dec_ref, beta_ref, lw_ref, small, rq, rk, rv, rs, kn, gm, wu, ab, cols, lrt, ot, tot, relay,
    st_send, st_recv, mt, wg, sib_send, sib_recv, x_send, x_recv, fsend, fin,
    kv_ss, kv_rs, st_ss, st_rs, o_ss, o_rs, w1_ss, w1_rs, w2_ss, w2_rs,
    sb_ss, sb_rs, x_ss, x_rs, f_ss, f_rs, in_s,
):
    net = Copies()
    ctx = lax.axis_index("ctx")
    head = lax.axis_index("head")
    zi = ctx // 8
    yi = ctx % 8
    yl = ctx % 4
    yh = yi // 4
    base = ctx - yl
    core = head % 2
    xi = head // 2

    def at_zy(z, y):
        return {"ctx": z * 8 + y}

    def lane(j):
        return pl.ds(pl.multiple_of(j * DK, DK), DK)

    barrier = pltpu.get_barrier_semaphore()
    for z in ((zi + 1) % 8, (zi + 7) % 8, zi ^ 2, zi ^ 4):
        pl.semaphore_signal(barrier, inc=1, device_id=at_zy(z, yi), device_id_type=MESH)
    pl.semaphore_signal(barrier, inc=1, device_id={"ctx": ctx ^ 4}, device_id_type=MESH)
    for d in range(1, 4):
        pl.semaphore_signal(
            barrier, inc=1, device_id={"ctx": base + (yl + d) % 4}, device_id_type=MESH
        )
    for d in (1, 3):
        pl.semaphore_signal(
            barrier, inc=1, device_id={"head": ((xi + d) % 4) * 2 + core}, device_id_type=MESH
        )
    pl.semaphore_signal(barrier, inc=1, device_id={"head": head ^ 1}, device_id_type=MESH)

    loads = [
        pltpu.make_async_copy(src, dst, in_s.at[i])
        for i, (src, dst) in enumerate(
            (
                (dec_hbm, dec_ref), (beta_hbm, beta_ref), (lw_hbm, lw_ref),
                (w_ref, wg.at[zi, yh]), (k_hbm, k_ref), (v_hbm, v_ref), (q_hbm, q_ref),
            )
        )
    ]
    for cp in loads:
        cp.start()

    for cp in loads[:3]:
        cp.wait()
    for j in range(4):
        small[j, 0:1, :] = dec_ref[j : j + 1]
        small[j, 1:2, :] = beta_ref[j : j + 1]
        for l in range(7):
            small[j, 2 + l : 3 + l, :] = lw_ref[l, j : j + 1]
        small[j, 9:16, :] = jnp.zeros((7, TB), F32)

    for cp in loads[3:]:
        cp.wait()
    pl.semaphore_wait(barrier, 11)

    def to_group(src, dst, a):
        copies = []
        for d in (3, 2, 1):
            to = (yl + d) % 4
            copies.append(
                pltpu.make_async_remote_copy(
                    src_ref=src.at[to] if a == 1 else src.at[:, lane(to)],
                    dst_ref=dst.at[yl], send_sem=kv_ss.at[a, d], recv_sem=kv_rs.at[a, d],
                    device_id={"ctx": base + to}, device_id_type=MESH,
                )
            )
        net.start(*copies)
        return copies

    k_copies = to_group(k_ref, rk, 0)
    s_copies = to_group(small, rs, 1)
    v_copies = to_group(v_ref, rv, 2)

    w_pair = pltpu.make_async_remote_copy(
        src_ref=wg.at[zi, yh], dst_ref=wg.at[zi, yh], send_sem=w1_ss, recv_sem=w1_rs,
        device_id={"ctx": ctx ^ 4}, device_id_type=MESH,
    )
    net.start(w_pair)

    def w_copy(sub, way, step):
        slot = (zi + (step - 1) * (2 * way - 1) + 8) % 8
        part = wg.at[slot, yh if sub == 0 else 1 - yh]
        if step == 4:
            part = part.at[pl.ds(32 * way, 32)]
        return pltpu.make_async_remote_copy(
            src_ref=part, dst_ref=part,
            send_sem=w2_ss.at[sub, way, step], recv_sem=w2_rs.at[sub, way, step],
            device_id=at_zy((zi + 1 + 6 * way) % 8, yi), device_id_type=MESH,
        )

    w_ring = [
        [[w_copy(sub, way, step) for way in range(2)] for step in range(1, 5)] for sub in range(2)
    ]

    def w_pass_on(sub, step):
        net.arrive(*w_ring[sub][step - 1])
        net.start(*w_ring[sub][step])

    net.start(*w_ring[0][0])

    rs[yl] = small[yl]
    rk[yl] = k_ref[:, lane(yl)]
    rv[yl] = v_ref[:, lane(yl)]
    rq[yl] = q_ref[:, lane(yl)]

    ri = lax.broadcasted_iota(jnp.int32, (TB, TB), 0)
    ci = lax.broadcasted_iota(jnp.int32, (TB, TB), 1)
    eye = (ri == ci).astype(F32)
    upto = (ri <= ci).astype(F32)

    def pairs(slots, values_here=None):
        n = len(slots)
        ls, keys, betas, tails, lasts = [], [], [], [], []
        for s in slots:
            sm = rs[s]
            g_rows = -jnp.dot(
                sm, upto, preferred_element_type=F32, precision=lax.Precision.HIGHEST
            )
            g_row = g_rows[0:1]
            col = jnp.concatenate([g_row, sm[1:8]], axis=0)
            col = jnp.concatenate([col, jnp.zeros((TB - 8, TB), F32)], axis=0).T
            g_col = col[:, 0:1]
            b_col = col[:, 1:2]
            growth = jnp.exp(g_col)
            g_last = g_row[:, TB - 1 : TB]
            ratio = jnp.where(ci <= ri, jnp.exp(jnp.minimum(g_col - g_row, 0.0)), 0.0)
            kk = unit_rows(rk[s].astype(F32))
            kn[s] = kk
            gm[s] = ratio
            cols[s] = jnp.broadcast_to(growth, (TB, DK))
            ls.append(jnp.where(ci < ri, b_col * ratio * dot3_nt(kk, kk), 0.0))
            keys.append((b_col * growth) * kk)
            betas.append(b_col)
            tails.append(jnp.exp(g_last - g_col) * kk)
            lasts.append(jnp.exp(g_last))
        inv = [eye - jnp.where((ri % 2 == 1) & (ci == ri - 1), l, 0.0) for l in ls]
        b = 2
        while b < TB:
            mask = ((ri // b) % 2 == 1) & (ci // b == ri // b - 1)
            mid = [dot3(inv[i], jnp.where(mask, ls[i], 0.0)) for i in range(n)]
            inv = [inv[i] - dot3(mid[i], inv[i]) for i in range(n)]
            b *= 2
        if values_here is not None:
            values_here()
        sol = [
            dot3(
                inv[i],
                jnp.concatenate([keys[i], betas[i] * rv[s].astype(F32)], axis=1),
            )
            for i, s in enumerate(slots)
        ]
        for i, s in enumerate(slots):
            wu[s] = sol[i]
            m = dot3(tails[i].T, sol[i])
            ab[s, :, 0:DK] = lasts[i] * eye - m[:, 0:DK]
            ab[s, :, DK:] = m[:, DK:]

    pairs([yl])
    w_pass_on(0, 1)

    net.arrive(*s_copies)
    net.arrive(*k_copies)
    q_copies = to_group(q_ref, rq, 3)
    w_pass_on(0, 2)

    def values_here():
        net.arrive(*v_copies)
        net.arrive(w_pair)
        net.start(*w_ring[1][0])

    pairs([(yl + d) % 4 for d in range(1, 4)], values_here)

    def apply(second, first):
        r = dot3(second[:, 0:DK], first)
        return jnp.concatenate([r[:, 0:DK], r[:, DK:] + second[:, DK:]], axis=1)

    ab01 = apply(ab[1], ab[0])
    ab23 = apply(ab[3], ab[2])
    group = apply(ab23, ab01)

    def level_copy(i):
        if i < 3:
            src, dst = st_send.at[i], st_recv.at[i]
        else:
            src, dst = st_send.at[i, :, pl.ds(DK, DK)], st_recv.at[i, :, pl.ds(DK, DK)]
        return pltpu.make_async_remote_copy(
            src_ref=src, dst_ref=dst, send_sem=st_ss.at[i], recv_sem=st_rs.at[i],
            device_id={"ctx": ctx ^ (4 << i)}, device_id_type=MESH,
        )

    levels = [level_copy(i) for i in range(4)]
    tot[...] = group
    st_send[0] = group.astype(BF16)
    net.start(levels[0])
    relay[...] = eye
    w_pass_on(1, 1)
    w_pass_on(0, 3)

    net.arrive(*q_copies)
    b01 = ab01[:, DK:]
    a2 = ab[2, :, 0:DK]
    r3 = dot3(a2, ab01)
    starts = [None, ab[0, :, 0:DK], ab01[:, 0:DK], r3[:, 0:DK]]
    for s in range(4):
        kk = kn[s]
        qq = unit_rows(rq[s].astype(F32))
        p = dot3_nt(qq, kk) * gm[s]
        pwu = dot3(p, wu[s])
        moved = cols[s] * qq - pwu[:, 0:DK]
        inner = pwu[:, DK:]
        wt = rs[s]
        o = wt[2:3] * inner.T
        if s == 0:
            lifted = moved
        elif s == 1:
            r = dot3(moved, ab[0])
            lifted = r[:, 0:DK]
            o = o + wt[3:4] * r[:, DK:].T
        elif s == 2:
            r = dot3(moved, ab01)
            lifted = r[:, 0:DK]
            o = o + wt[4:5] * r[:, DK:].T
        else:
            r = dot3(moved, jnp.concatenate([r3, ab[2, :, DK:]], axis=1))
            lifted = r[:, 0:DK]
            o = o + wt[4:5] * r[:, DK : 2 * DK].T + wt[3:4] * r[:, 2 * DK :].T
        lrt[:, s * TB : (s + 1) * TB] = lifted.T
        ot[:, s * TB : (s + 1) * TB] = o

    def add_level(i, state, lifted=None):
        t = dot3(state.T, lrt[...] if lifted is None else lifted)
        for s in range(4):
            sl = slice(s * TB, (s + 1) * TB)
            ot[:, sl] = ot[:, sl] + rs[s, 4 + i + 1 : 4 + i + 2, :] * t[:, sl]

    for i in range(4):
        upper = (ctx // (4 << i)) % 2 == 1
        if i < 3:
            net.arrive(levels[i])
            other = st_recv[i].astype(F32)
            own = tot[...]
            first = jnp.where(upper, other, own)
            second = jnp.where(upper, own, other)
            old = relay[...]
            r = dot3(jnp.concatenate([second[:, 0:DK], old], axis=0), first)
            new_b = r[0:DK, DK:] + second[:, DK:]
            tot[:, 0:DK] = r[0:DK, 0:DK]
            tot[:, DK:] = new_b
            st_send[i + 1, :, 0:DK] = r[0:DK, 0:DK].astype(BF16)
            st_send[i + 1, :, DK:] = new_b.astype(BF16)
            if i < 2:
                net.start(levels[i + 1])
            else:
                @pl.when((ctx // 32) % 2 == 0)
                def _():
                    levels[3].start()
            relay[...] = jnp.where(upper, r[DK:, 0:DK], old)

            @pl.when(upper)
            def _():
                add_level(i, r[DK:, DK:])

            if i < 2:
                w_pass_on(1, 2 + i)
        else:
            @pl.when(upper)
            def _():
                lifted = dot3(relay[...].T, lrt[...])
                levels[3].wait_recv()
                add_level(3, st_recv[3, :, DK:].astype(F32), lifted)

            @pl.when(jnp.logical_not(upper))
            def _():
                levels[3].wait_send()

    mine = mt.at[pl.ds(pl.multiple_of(yl * DK, DK), DK)]
    mine[...] = ot[...].astype(BF16)
    o_copies = []
    for d in (3, 2, 1):
        cp = pltpu.make_async_remote_copy(
            src_ref=mine, dst_ref=mine, send_sem=o_ss.at[d], recv_sem=o_rs.at[d],
            device_id={"ctx": base + (yl + d) % 4}, device_id_type=MESH,
        )
        net.start(cp)
        o_copies.append(cp)
    net.arrive(*w_ring[0][3])
    net.arrive(*w_ring[1][3])
    net.arrive(*o_copies)

    def share(block):
        w = wg[block].reshape(128, 512)
        return jnp.dot(w, mt[...], preferred_element_type=F32)

    sib, xs = {}, []

    def to_sibling(d):
        sib_send[d] = share(((xi + d) % 4) * 2 + 1 - core).astype(BF16)
        sib[d] = pltpu.make_async_remote_copy(
            src_ref=sib_send.at[d], dst_ref=sib_recv.at[d], send_sem=sb_ss.at[d], recv_sem=sb_rs.at[d],
            device_id={"head": head ^ 1}, device_id_type=MESH,
        )
        net.start(sib[d])

    def chip_sum(d):
        own = share(((xi + d) % 4) * 2 + core)
        net.arrive(sib[d])
        return own + sib_recv[d].astype(F32)

    def x_copy(i, src, way):
        return pltpu.make_async_remote_copy(
            src_ref=src, dst_ref=x_recv.at[i], send_sem=x_ss.at[i], recv_sem=x_rs.at[i],
            device_id={"head": ((xi + 1 + 2 * way) % 4) * 2 + core}, device_id_type=MESH,
        )

    halves = (pl.ds(0, 64), pl.ds(64, 64))
    x_far = [x_copy(way, x_send.at[2, halves[way]], way) for way in range(2)]
    x_plain = [x_copy(2 + way, x_send.at[1 + 2 * way, halves[1 - way]], way) for way in range(2)]
    x_added = [x_copy(4 + way, x_send.at[1 + 2 * way, halves[way]], way) for way in range(2)]

    def to_neighbour(way):
        near = chip_sum(1 + 2 * way)
        keep, add = (near[64:], near[:64]) if way == 0 else (near[:64], near[64:])
        x_send[1 + 2 * way, halves[1 - way], :] = keep.astype(BF16)
        net.start(x_plain[way])
        return add

    def pass_added(way, add):
        net.arrive(x_far[way])
        x_send[1 + 2 * way, halves[way], :] = (add + x_recv[way].astype(F32)).astype(BF16)
        net.start(x_added[way])

    for d in (2, 1, 3, 0):
        to_sibling(d)
    x_send[2] = chip_sum(2).astype(BF16)
    net.start(*x_far)
    add0 = to_neighbour(0)
    add1 = to_neighbour(1)
    total = chip_sum(0)
    pass_added(0, add0)
    pass_added(1, add1)
    net.arrive(*x_plain, *x_added)
    low = x_recv[3].astype(F32) + x_recv[4].astype(F32)
    high = x_recv[2].astype(F32) + x_recv[5].astype(F32)
    total = total + jnp.concatenate([low, high], axis=0)

    fsend[...] = total.astype(BF16)
    fcopies = []
    for d in (3, 2, 1):
        cp = pltpu.make_async_remote_copy(
            src_ref=fsend.at[:, lane((yl + d) % 4)], dst_ref=fin.at[yl],
            send_sem=f_ss.at[d], recv_sem=f_rs.at[d],
            device_id={"ctx": base + (yl + d) % 4}, device_id_type=MESH,
        )
        net.start(cp)
        fcopies.append(cp)
    fin[yl] = fsend[:, lane(yl)]
    net.arrive(*fcopies)
    parts = [fin[j, 64 * m : 64 * m + 64, :] for m in range(2) for j in range(4)]
    out_ref[...] = jnp.concatenate(parts, axis=0).astype(F32).T.astype(BF16)

    net.finish()


def per_device(q, k, v, dec, beta, lw, w):
    vmem = pl.BlockSpec(memory_space=pltpu.VMEM)
    dma = pltpu.SemaphoreType.DMA
    return pl.pallas_call(
        kernel,
        out_shape=jax.ShapeDtypeStruct((TB, 512), BF16),
        in_specs=[pl.BlockSpec(memory_space=pltpu.HBM)] * 7,
        out_specs=vmem,
        scratch_shapes=[
            pltpu.VMEM((TB, 4 * DK), BF16),
            pltpu.VMEM((TB, 4 * DK), BF16),
            pltpu.VMEM((TB, 4 * DK), BF16),
            pltpu.VMEM((4, TB), F32),
            pltpu.VMEM((4, TB), F32),
            pltpu.VMEM((7, 4, TB), F32),
            pltpu.VMEM((4, 16, TB), F32),
            pltpu.VMEM((4, TB, DK), BF16),
            pltpu.VMEM((4, TB, DK), BF16),
            pltpu.VMEM((4, TB, DK), BF16),
            pltpu.VMEM((4, 16, TB), F32),
            pltpu.VMEM((4, TB, DK), F32),
            pltpu.VMEM((4, TB, TB), F32),
            pltpu.VMEM((4, TB, 2 * DK), F32),
            pltpu.VMEM((4, DK, 2 * DK), F32),
            pltpu.VMEM((4, TB, DK), F32),
            pltpu.VMEM((DK, 4 * TB), F32),
            pltpu.VMEM((DK, 4 * TB), F32),
            pltpu.VMEM((DK, 2 * DK), F32),
            pltpu.VMEM((DK, DK), F32),
            pltpu.VMEM((4, DK, 2 * DK), BF16),
            pltpu.VMEM((4, DK, 2 * DK), BF16),
            pltpu.VMEM((4 * DK, 4 * TB), BF16),
            pltpu.VMEM((8, 2, 64, 512), BF16),
            pltpu.VMEM((4, DK, 4 * TB), BF16),
            pltpu.VMEM((4, DK, 4 * TB), BF16),
            pltpu.VMEM((4, DK, 4 * TB), BF16),
            pltpu.VMEM((6, 64, 4 * TB), BF16),
            pltpu.VMEM((DK, 4 * TB), BF16),
            pltpu.VMEM((4, DK, TB), BF16),
            dma((4, 4)), dma((4, 4)), dma((4,)), dma((4,)),
            dma((4,)), dma((4,)), dma, dma, dma((2, 2, 5)), dma((2, 2, 5)),
            dma((4,)), dma((4,)), dma((6,)), dma((6,)), dma((4,)), dma((4,)), dma((7,)),
        ],
        compiler_params=pltpu.CompilerParams(
            collective_id=0, has_side_effects=True, vmem_limit_bytes=60 * 2**20
        ),
        name="mixer",
    )(q, k, v, dec.T, beta.T, lw.transpose(2, 1, 0), w.T)


def solution(mesh):
    spec = P("ctx", "head")
    return jax.shard_map(
        per_device,
        mesh=mesh,
        in_specs=(spec,) * 5 + (P("ctx", "head", None), P("head", "ctx")),
        out_specs=spec,
        check_vma=False,
    )
```
